256 devices in a mesh: sx: 32 (over x, y, core), sy: 8 (over z).
Axes of the slice: x: 4, y: 4, z: 8, core: 2. Of those that a mesh axis runs over, the one named last changes fastest.
Arguments:
- start_block: float32 [64, 1048576], P(None, ('sx', 'sy'))
- blocks: float32 [7, 64, 1048576], P(None, None, ('sx', 'sy')), may hold values from -0.25 to 0.25
- neighbors: int32 [6, 16384], P(None, ('sx', 'sy')), may hold values from 0 to 95, as said below
- ghost_lists: int32 [32, 8, 4, 8], P('sx', 'sy'), may hold values from 0 to 63, as said below
Outputs:
- q_basis: float32 [192, 1048576], P(None, ('sx', 'sy'))
- r_factor: float32 [192, 192], replicated
The draws below stay inside these ranges and needn't reach their ends.
Inputs may be any that keep to these rules, and one draw needn't show every extreme that they name: `neighbors`: values 0 to 63 name a local element; 64 + d * 8 + g names ghost slot g of direction d. Every ghost slot is named by some entry of every subdomain. `ghost_lists`: the 8 entries of one list are distinct.
All inputs are finite; a program needn't handle non-finite values.
Results may differ from the reference program's by a relative error of at most 0.00016.
Values sent between devices are 32-bit elements; how exact they have to be, the bound alone decides.
A program may use at most 192 MiB of HBM per device.

```python
import math
import jax
import jax.numpy as jnp
from jax import lax

NB = 64
RHS = 64
ELEM_DEV = 64
GHOSTS = 8
NROWS = 1048576
N_SX = 32
N_SY = 8


def draw_start_block(key, part):
    key = jax.random.fold_in(key, 11)
    first, second = jax.random.split(key, 2)
    elems = ELEM_DEV * N_SX * N_SY
    rows = elems * NB
    noise = jnp.clip(jax.random.normal(first, (RHS, rows), jnp.float32), -5.0, 5.0)
    level = jnp.exp(jax.random.uniform(second, (elems, 1), jnp.float32, math.log(0.3), math.log(3.0)))
    level = jnp.broadcast_to(level, (elems, NB)).reshape(1, rows)
    ramp = 1.0 + 2.0 * jnp.arange(rows, dtype=jnp.float32)[None, :] / (rows - 1)
    return noise * level * ramp


def one_pattern(key):
    first, second = jax.random.split(key)
    count = 6 * ELEM_DEV
    spots = jax.random.permutation(first, count)[:4 * GHOSTS]
    values = jax.random.randint(second, (count,), 0, ELEM_DEV + 4 * GHOSTS)
    values = values.at[spots].set(ELEM_DEV + jnp.arange(4 * GHOSTS, dtype=jnp.int32))
    return values.reshape(ELEM_DEV, 6)


def draw_neighbors(key, part):
    key = jax.random.fold_in(key, 23)
    keys = jax.random.split(key, N_SX * N_SY)
    patterns = jax.vmap(one_pattern)(keys)
    return jnp.transpose(patterns, (2, 0, 1)).reshape(6, N_SX * N_SY * ELEM_DEV).astype(jnp.int32)


def one_list(key):
    return jax.random.permutation(key, ELEM_DEV)[:GHOSTS]


def draw_ghost_lists(key, part):
    key = jax.random.fold_in(key, 37)
    keys = jax.random.split(key, N_SX * N_SY * 4)
    lists = jax.vmap(one_list)(keys)
    return lists.reshape(N_SX, N_SY, 4, GHOSTS).astype(jnp.int32)


def block_levels(rng, shape, pieces, smallest, largest):
    factor_of = 1.0
    for position, shards_of in pieces:
        draws = jax.random.uniform(jax.random.fold_in(jax.random.fold_in(rng, 6), position), (shards_of,), jnp.float32, smallest / len(pieces), largest / len(pieces))
        factor_of = factor_of * jnp.repeat(jnp.exp(draws), shape[position] // shards_of).reshape((-1,) + (1,) * (len(shape) - 1 - position))
    return factor_of


def centred(stream_key, shape, deviation, limit, cuts=(), kind=jnp.bfloat16):
    array = deviation * jax.random.normal(stream_key, shape, jnp.float32)
    if cuts:
        array = array * block_levels(stream_key, shape, cuts, -0.22, 0.18)
    return jnp.clip(array, -limit, limit).astype(kind)


def setup_inputs(seed: int = 0) -> dict:
    key_list = jax.random.split(jax.random.key(seed), 5)
    start_block = draw_start_block(jax.random.fold_in(key_list[4], 71), 0)
    blocks = centred(key_list[1], (7, NB, NROWS), (7 * NB) ** -0.5, 0.25, ((2, 256),), jnp.float32)
    neighbors = draw_neighbors(jax.random.fold_in(key_list[4], 71), 0)
    ghost_lists = draw_ghost_lists(jax.random.fold_in(key_list[4], 71), 0)
    return dict(start_block=start_block, blocks=blocks, neighbors=neighbors, ghost_lists=ghost_lists)


def apply_operator(vec, blocks, neighbors, ghost_lists):
    grid = vec.reshape(RHS, N_SX, N_SY, ELEM_DEV, NB)
    received = []
    for direction, (axis_pos, step) in enumerate(((1, 1), (1, -1), (2, 1), (2, -1))):
        listed = ghost_lists[:, :, direction, :].astype(jnp.int32)
        sent = jnp.take_along_axis(grid, listed[None, :, :, :, None], axis=3)
        received.append(jnp.roll(sent, step, axis=axis_pos))
    extended = jnp.concatenate([grid] + received, axis=3)
    columns = neighbors.astype(jnp.int32).reshape(6, N_SX, N_SY, ELEM_DEV)
    own_index = jnp.broadcast_to(jnp.arange(ELEM_DEV, dtype=jnp.int32), (N_SX, N_SY, ELEM_DEV))
    tiles = blocks.reshape(7, NB, N_SX, N_SY, ELEM_DEV, NB)
    total = jnp.zeros((RHS, N_SX, N_SY, ELEM_DEV, NB), jnp.float32)
    for slot in range(7):
        index = own_index if slot == 0 else columns[slot - 1]
        picked = jnp.take_along_axis(extended, index[None, :, :, :, None], axis=3)
        total = total + jnp.einsum('zxyec,cxyer->zxyer', picked, tiles[slot], precision=lax.Precision.HIGHEST)
    return total.reshape(RHS, NROWS)

def reference(start_block, blocks, neighbors, ghost_lists):
    power_one = apply_operator(start_block, blocks, neighbors, ghost_lists)
    power_two = apply_operator(power_one, blocks, neighbors, ghost_lists)
    basis = jnp.concatenate([start_block, power_one, power_two], axis=0)
    gram = jnp.dot(basis, basis.T, precision=lax.Precision.HIGHEST)
    lower = jnp.linalg.cholesky(gram)
    orthonormal = jax.scipy.linalg.solve_triangular(lower, basis, lower=True)
    scale = jnp.sqrt(jnp.float32(NROWS))
    return (orthonormal * scale, lower.T / scale)
```

```python
import functools
import math

import jax
import jax.numpy as jnp
from jax import lax
from jax.experimental import pallas as pl
from jax.experimental.pallas import tpu as pltpu
from jax.sharding import PartitionSpec as P

MESH = pl.DeviceIdType.MESH
F32 = jnp.float32
BF16 = jnp.bfloat16
HIGHEST = lax.Precision.HIGHEST


def split(value):
    high = value.astype(BF16)
    low = (value - high.astype(F32)).astype(BF16)
    return high, low


def exact_dot(a, b, contract):
    return lax.dot_general(a, b, ((contract[0:1], contract[1:2]), ((), ())), precision=HIGHEST, preferred_element_type=F32)


def factor(matrix):
    size = matrix.shape[0]
    rows = lax.broadcasted_iota(jnp.int32, (size, size), 0)
    cols = lax.broadcasted_iota(jnp.int32, (size, size), 1)
    wide = jnp.concatenate([matrix, jnp.where(rows == cols, 1.0, 0.0).astype(F32)], axis=1)
    parts = [wide[8 * b:8 * b + 8] for b in range(size // 8)]
    sub = lax.broadcasted_iota(jnp.int32, (8, 2 * size), 0)
    lane = lax.broadcasted_iota(jnp.int32, (8, 2 * size), 1)
    for j in range(size):
        home, at = j // 8, j % 8
        pivot_row = jnp.broadcast_to(parts[home][at:at + 1], (8, 2 * size))
        pivot = jnp.broadcast_to(parts[home][at:at + 1, j:j + 1], (8, 2 * size))
        scaled = pivot_row / pivot
        for b in range(home, size // 8):
            column = jnp.broadcast_to(parts[b][:, j:j + 1], (8, 2 * size))
            if b == home:
                column = jnp.where(sub > at, column, 0.0)
            parts[b] = parts[b] - column * scaled
    done = []
    for b in range(size // 8):
        diagonal = jnp.sum(jnp.where(lane == sub + 8 * b, parts[b], 0.0), axis=1, keepdims=True)
        scaled = parts[b] / jnp.sqrt(diagonal)
        done.append(jnp.where((lane < sub + 8 * b), 0.0, scaled))
    result = jnp.concatenate(done, axis=0)
    return result[:, :size], result[:, size:]


def basis_kernel(n_sx, n_sy, start_hbm, blocks_hbm, near_ref, lists_ref, high_hbm, low_hbm, upper_ref, inverse_ref,
                 start_vm, stage, tiles, ext_a, ext_b, high, low, send, recv, gram, chunks, mine, planes, whole,
                 start_sem, block_sem, out_sem, send_sem, recv_sem, sum_send, sum_recv):
    sx, sy = lax.axis_index("sx"), lax.axis_index("sy")
    count_rhs, rows = start_hbm.shape
    pairs = rows // 128
    groups = block_sem.shape[0]
    width = rows // groups
    per_group = width // 128

    start_copy = pltpu.make_async_copy(start_hbm, start_vm, start_sem)
    start_copy.start()
    block_copies = []
    for c in range(groups):
        copy = pltpu.make_async_copy(blocks_hbm.at[:, :, pl.ds(c * width, width)], stage.at[:, :, pl.ds(c * width, width)], block_sem.at[c])
        copy.start()
        block_copies.append(copy)

    barrier = pltpu.get_barrier_semaphore()

    @pl.loop(1, n_sx)
    def _(d):
        pl.semaphore_signal(barrier, inc=1, device_id=(lax.rem(sx + d, n_sx), sy), device_id_type=MESH)

    @pl.loop(1, n_sy)
    def _(d):
        pl.semaphore_signal(barrier, inc=1, device_id=(sx, lax.rem(sy + d, n_sy)), device_id_type=MESH)

    left_half = lax.broadcasted_iota(jnp.int32, (count_rhs, 128), 1) < 64

    def spread(pair, ext, slot):
        turned = pltpu.roll(pair, 64, 1)
        for side, both in enumerate((jnp.where(left_half, pair, turned), jnp.where(left_half, turned, pair))):
            h, l = split(both)
            ext[slot + side, 0] = h
            ext[slot + side, 1] = l

    def keep(pair, p, power):
        h, l = split(pair)
        at = pl.ds(pl.multiple_of(p * 128, 128), 128)
        high[power * count_rhs:(power + 1) * count_rhs, at] = h
        low[power * count_rhs:(power + 1) * count_rhs, at] = l

    def exchange(ext, turn):
        targets = (
            (lax.rem(sx + 1, n_sx), sy),
            (lax.rem(sx + n_sx - 1, n_sx), sy),
            (sx, lax.rem(sy + 1, n_sy)),
            (sx, lax.rem(sy + n_sy - 1, n_sy)),
        )
        copies = []
        for d in (2, 3, 0, 1):
            for g in range(4):
                first, second = lists_ref[0, 0, d, 2 * g], lists_ref[0, 0, d, 2 * g + 1]
                one = ext[first, 0].astype(F32) + ext[first, 1].astype(F32)
                two = ext[second, 0].astype(F32) + ext[second, 1].astype(F32)
                send[turn, d, g] = jnp.where(left_half, one, two)
            if turn == 0 and d == 2:
                pl.semaphore_wait(barrier, n_sx + n_sy - 2)
            copy = pltpu.make_async_remote_copy(
                src_ref=send.at[turn, d], dst_ref=recv.at[turn, d],
                send_sem=send_sem.at[turn, d], recv_sem=recv_sem.at[turn, d],
                device_id=targets[d], device_id_type=MESH)
            copy.start()
            copies.append((d, copy))
        return copies

    def arrive(copies, ext, turn):
        for d, copy in copies:
            copy.wait()
            for g in range(4):
                spread(recv[turn, d, g], ext, 64 + d * 8 + 2 * g)

    def power(ext, use):
        @pl.loop(0, pairs)
        def _(p):
            lhs = []
            for hl in range(2):
                for side in range(2):
                    e = 2 * p + side
                    slots = [e] + [near_ref[k, e] for k in range(6)] + [near_ref[5, e]]
                    lhs.append(jnp.concatenate(
                        [jnp.where(left_half, ext[slots[2 * k], hl], ext[slots[2 * k + 1], hl]) for k in range(4)], axis=1))
            out = jnp.dot(jnp.concatenate(lhs, axis=0), tiles[p], preferred_element_type=F32)
            out = out[:, :128] + out[:, 128:]
            out = out[:2 * count_rhs] + out[2 * count_rhs:]
            use(p, jnp.where(left_half, out[:count_rhs], out[count_rhs:]))

    start_copy.wait()

    @pl.loop(0, pairs)
    def _(p):
        pair = start_vm[:, pl.ds(pl.multiple_of(p * 128, 128), 128)]
        keep(pair, p, 0)
        spread(pair, ext_a, 2 * p)

    copies = exchange(ext_a, 0)

    for c in range(groups):
        block_copies[c].wait()

        @pl.loop(c * per_group, (c + 1) * per_group)
        def _(p):
            at = pl.ds(pl.multiple_of(p * 128, 128), 128)
            for k in range(7):
                h, l = split(stage[k, :, at])
                tiles[p, k * 64:(k + 1) * 64, 0:128] = h
                tiles[p, k * 64:(k + 1) * 64, 128:256] = l
            tiles[p, 448:512, :] = jnp.zeros((64, 256), BF16)

    arrive(copies, ext_a, 0)

    def first(p, pair):
        keep(pair, p, 1)
        spread(pair, ext_b, 2 * p)

    power(ext_a, first)
    copies = exchange(ext_b, 1)
    arrive(copies, ext_b, 1)
    power(ext_b, lambda p, pair: keep(pair, p, 2))

    out_copies = [pltpu.make_async_copy(high, high_hbm, out_sem.at[0]), pltpu.make_async_copy(low, low_hbm, out_sem.at[1])]
    for copy in out_copies:
        copy.start()

    size = 3 * count_rhs
    depth = 1024

    def inner(c, totals):
        at = pl.ds(pl.multiple_of(c * depth, depth), depth)
        h, l = high[:, at], low[:, at]
        dims = (((1,), (1,)), ((), ()))
        return (totals[0] + lax.dot_general(h, h, dims, preferred_element_type=F32),
                totals[1] + lax.dot_general(h, l, dims, preferred_element_type=F32))

    zero = jnp.zeros((size, size), F32)
    straight, crossed = lax.fori_loop(0, rows // depth, inner, (zero, zero))
    local = straight + crossed + crossed.T
    per = gram.shape[1]
    gram[0:size // per] = local[:, :128].reshape(size // per, per, 128)
    corner = jnp.concatenate([local[128:, 128:], jnp.zeros((count_rhs, 128 - count_rhs), F32)], axis=1)
    gram[size // per:] = corner.reshape(count_rhs // per, per, 128)

    @pl.loop(1, n_sx)
    def _(d):
        other = lax.rem(sx + d, n_sx)
        pltpu.make_async_remote_copy(
            src_ref=gram.at[other], dst_ref=chunks.at[d - 1], send_sem=sum_send.at[0], recv_sem=sum_recv.at[0],
            device_id=(other, sy), device_id_type=MESH).start()

    pltpu.make_async_copy(chunks, chunks, sum_recv.at[0]).wait()
    part = gram[sx]
    for d in range(n_sx - 1):
        part = part + chunks[d]
    mine[...] = part
    planes[sy] = part

    @pl.loop(1, n_sy)
    def _(d):
        pltpu.make_async_remote_copy(
            src_ref=mine, dst_ref=planes.at[sy], send_sem=sum_send.at[1], recv_sem=sum_recv.at[1],
            device_id=(sx, lax.rem(sy + d, n_sy)), device_id_type=MESH).start()

    pltpu.make_async_copy(planes.at[pl.ds(0, n_sy - 1)], planes.at[pl.ds(0, n_sy - 1)], sum_recv.at[1]).wait()
    pltpu.make_async_copy(planes.at[pl.ds(0, n_sy - 1)], planes.at[pl.ds(0, n_sy - 1)], sum_send.at[1]).wait()
    part = planes[0]
    for d in range(1, n_sy):
        part = part + planes[d]
    mine[...] = part
    whole[sx] = part

    @pl.loop(1, n_sx)
    def _(d):
        pltpu.make_async_remote_copy(
            src_ref=mine, dst_ref=whole.at[sx], send_sem=sum_send.at[2], recv_sem=sum_recv.at[2],
            device_id=(lax.rem(sx + d, n_sx), sy), device_id_type=MESH).start()

    pltpu.make_async_copy(whole.at[pl.ds(0, n_sx - 1)], whole.at[pl.ds(0, n_sx - 1)], sum_recv.at[2]).wait()
    full = whole[...].reshape(n_sx * per, 128)

    u00, x00 = factor(full[0:64, 0:64])
    u01 = exact_dot(x00, full[0:64, 64:128], (1, 0))
    u11, x11 = factor(full[64:128, 64:128] - exact_dot(u01, u01, (0, 0)))
    x10 = -exact_dot(x11, exact_dot(u01, x00, (0, 0)), (1, 0))
    none = jnp.zeros((64, 64), F32)
    x1 = jnp.concatenate([jnp.concatenate([x00, none], axis=1), jnp.concatenate([x10, x11], axis=1)], axis=0)
    u2 = exact_dot(x1, full[128:192], (1, 1))
    u22, x22 = factor(full[192:256, 0:64] - exact_dot(u2, u2, (0, 0)))
    x2 = -exact_dot(x22, exact_dot(u2, x1, (0, 0)), (1, 0))
    upper_ref[0:64, 0:128] = jnp.concatenate([u00, u01], axis=1)
    upper_ref[64:128, 0:128] = jnp.concatenate([none, u11], axis=1)
    upper_ref[128:192, 0:128] = jnp.zeros((64, 128), F32)
    upper_ref[0:128, 128:192] = u2
    upper_ref[128:192, 128:192] = u22
    inverse_ref[0:128, 0:128] = x1
    inverse_ref[128:192, 0:128] = x2
    inverse_ref[0:128, 128:192] = jnp.zeros((128, 64), F32)
    inverse_ref[128:192, 128:192] = x22

    for copy in out_copies:
        copy.wait()
    pltpu.make_async_copy(chunks, chunks, sum_send.at[0]).wait()
    pltpu.make_async_copy(chunks, chunks, sum_send.at[2]).wait()


def result_kernel(scale, high_ref, low_ref, upper_ref, inverse_ref, q_ref, r_ref):
    xh, xl = split(inverse_ref[...] * scale)
    both = jnp.concatenate([xh, xl], axis=0)
    size = xh.shape[0]
    out = jnp.dot(both, high_ref[...], preferred_element_type=F32)
    q_ref[...] = out[:size] + out[size:] + jnp.dot(xh, low_ref[...], preferred_element_type=F32)
    r_ref[...] = upper_ref[...] / scale


def shards(n_sx, n_sy, start_block, blocks, neighbors, ghost_lists):
    count_rhs, rows = start_block.shape
    size = 3 * count_rhs
    pairs = rows // 128
    per = 256 // n_sx
    groups = 8
    anywhere = pl.BlockSpec(memory_space=pl.ANY)
    scalars = pl.BlockSpec(memory_space=pltpu.SMEM)
    vmem = pl.BlockSpec(memory_space=pltpu.VMEM)
    high, low, upper, inverse = pl.pallas_call(
        functools.partial(basis_kernel, n_sx, n_sy),
        out_shape=(
            jax.ShapeDtypeStruct((size, rows), BF16),
            jax.ShapeDtypeStruct((size, rows), BF16),
            jax.ShapeDtypeStruct((size, size), F32),
            jax.ShapeDtypeStruct((size, size), F32),
        ),
        in_specs=[anywhere, anywhere, scalars, scalars],
        out_specs=(anywhere, anywhere, vmem, vmem),
        scratch_shapes=[
            pltpu.VMEM((count_rhs, rows), F32),
            pltpu.VMEM((7, 64, rows), F32),
            pltpu.VMEM((pairs, 512, 256), BF16),
            pltpu.VMEM((96, 2, count_rhs, 128), BF16),
            pltpu.VMEM((96, 2, count_rhs, 128), BF16),
            pltpu.VMEM((size, rows), BF16),
            pltpu.VMEM((size, rows), BF16),
            pltpu.VMEM((2, 4, 4, count_rhs, 128), F32),
            pltpu.VMEM((2, 4, 4, count_rhs, 128), F32),
            pltpu.VMEM((n_sx, per, 128), F32),
            pltpu.VMEM((n_sx - 1, per, 128), F32),
            pltpu.VMEM((per, 128), F32),
            pltpu.VMEM((n_sy, per, 128), F32),
            pltpu.VMEM((n_sx, per, 128), F32),
            pltpu.SemaphoreType.DMA,
            pltpu.SemaphoreType.DMA((groups,)),
            pltpu.SemaphoreType.DMA((2,)),
            pltpu.SemaphoreType.DMA((2, 4)),
            pltpu.SemaphoreType.DMA((2, 4)),
            pltpu.SemaphoreType.DMA((3,)),
            pltpu.SemaphoreType.DMA((3,)),
        ],
        compiler_params=pltpu.CompilerParams(
            collective_id=0, has_side_effects=True, vmem_limit_bytes=48 * 1024 * 1024),
        name="basis_and_factor",
    )(start_block, blocks, neighbors, ghost_lists)

    scale = math.sqrt(rows * n_sx * n_sy)
    tile = 1024
    return pl.pallas_call(
        functools.partial(result_kernel, scale),
        grid=(rows // tile,),
        out_shape=(jax.ShapeDtypeStruct((size, rows), F32), jax.ShapeDtypeStruct((size, size), F32)),
        in_specs=[
            pl.BlockSpec((size, tile), lambda i: (0, i)),
            pl.BlockSpec((size, tile), lambda i: (0, i)),
            pl.BlockSpec((size, size), lambda i: (0, 0)),
            pl.BlockSpec((size, size), lambda i: (0, 0)),
        ],
        out_specs=(pl.BlockSpec((size, tile), lambda i: (0, i)), pl.BlockSpec((size, size), lambda i: (0, 0))),
        compiler_params=pltpu.CompilerParams(vmem_limit_bytes=32 * 1024 * 1024),
        name="orthonormal_rows",
    )(high, low, upper, inverse)


def solution(mesh):
    return jax.shard_map(
        functools.partial(shards, mesh.shape["sx"], mesh.shape["sy"]),
        mesh=mesh,
        in_specs=(
            P(None, ("sx", "sy")),
            P(None, None, ("sx", "sy")),
            P(None, ("sx", "sy")),
            P("sx", "sy", None, None),
        ),
        out_specs=(P(None, ("sx", "sy")), P()),
        check_vma=False,
    )
```

```python
import functools
import math

import jax
import jax.numpy as jnp
from jax import lax
from jax.experimental import pallas as pl
from jax.experimental.pallas import tpu as pltpu
from jax.sharding import PartitionSpec as P

MESH = pl.DeviceIdType.MESH
F32 = jnp.float32
BF16 = jnp.bfloat16
HIGHEST = lax.Precision.HIGHEST


def split(value):
    high = value.astype(BF16)
    low = (value - high.astype(F32)).astype(BF16)
    return high, low


def exact_dot(a, b, contract):
    return lax.dot_general(a, b, ((contract[0:1], contract[1:2]), ((), ())), precision=HIGHEST, preferred_element_type=F32)


def factor(matrix):
    size = matrix.shape[0]
    shape = (8, 2 * size)
    count = size // 8
    rows = lax.broadcasted_iota(jnp.int32, (size, size), 0)
    cols = lax.broadcasted_iota(jnp.int32, (size, size), 1)
    wide = jnp.concatenate([matrix, jnp.where(rows == cols, 1.0, 0.0).astype(F32)], axis=1)
    parts = [wide[8 * b:8 * b + 8] for b in range(count)]
    sub = lax.broadcasted_iota(jnp.int32, shape, 0)
    lane = lax.broadcasted_iota(jnp.int32, shape, 1)
    done = []
    for t in range(count):
        spread_cols = [[jnp.broadcast_to(parts[b][:, 8 * t + k:8 * t + k + 1], shape) for b in range(t, count)] for k in range(8)]
        spread_rows = [jnp.broadcast_to(parts[t][i:i + 1], shape) for i in range(8)]
        entry = [[jnp.broadcast_to(spread_cols[k][0][i:i + 1], shape) for k in range(i + 1)] for i in range(8)]
        inverse = []
        for j in range(8):
            inverse.append(1.0 / entry[j][j])
            ratio = [None] * 8
            for i in range(j + 1, 8):
                ratio[i] = entry[i][j] * inverse[j]
                for k in range(j + 1, i + 1):
                    entry[i][k] = entry[i][k] - ratio[i] * entry[k][j]
                spread_rows[i] = spread_rows[i] - ratio[i] * spread_rows[j]
                for b in range(1, count - t):
                    spread_cols[i][b] = spread_cols[i][b] - ratio[i] * spread_cols[j][b]
            scaled = spread_rows[j] * inverse[j]
            for b in range(1, count - t):
                parts[t + b] = parts[t + b] - spread_cols[j][b] * scaled
        own = spread_rows[0] / jnp.sqrt(entry[0][0])
        for i in range(1, 8):
            own = jnp.where(sub == i, spread_rows[i] / jnp.sqrt(entry[i][i]), own)
        done.append(jnp.where(lane < sub + 8 * t, 0.0, own))
    result = jnp.concatenate(done, axis=0)
    return result[:, :size], result[:, size:]


def add_up(parts):
    while len(parts) > 1:
        parts = [parts[i] + parts[i + 1] if i + 1 < len(parts) else parts[i] for i in range(0, len(parts), 2)]
    return parts[0]


class SumOverDevices:
    def __init__(self, shape, place, refs, send_sem, recv_sem):
        self.n_sx, self.n_sy = shape
        self.sx, self.sy = place
        self.local, self.chunks, self.planes, self.whole = refs
        self.send_sem, self.recv_sem = send_sem, recv_sem

    def send(self, round_, source, target, device):
        pltpu.make_async_remote_copy(
            src_ref=source, dst_ref=target, send_sem=self.send_sem.at[round_], recv_sem=self.recv_sem.at[round_],
            device_id=device, device_id_type=MESH).start()

    def spans(self):
        return (self.chunks, self.planes.at[pl.ds(0, self.n_sy - 1)], self.whole.at[pl.ds(0, self.n_sx - 1)])

    def arrived(self, round_):
        span = self.spans()[round_]
        pltpu.make_async_copy(span, span, self.recv_sem.at[round_]).wait()

    def scatter(self, value):
        self.local[...] = value.reshape(self.local.shape)

        @pl.loop(1, self.n_sx)
        def _(d):
            other = lax.rem(self.sx + d, self.n_sx)
            self.send(0, self.local.at[other], self.chunks.at[d - 1], (other, self.sy))

    def exchange(self):
        self.arrived(0)
        self.planes[self.sy] = add_up([self.local[self.sx]] + [self.chunks[d] for d in range(self.n_sx - 1)])

        @pl.loop(1, self.n_sy)
        def _(d):
            mine = self.planes.at[self.sy]
            self.send(1, mine, mine, (self.sx, lax.rem(self.sy + d, self.n_sy)))

    def gather(self):
        self.arrived(1)
        self.whole[self.sx] = add_up([self.planes[d] for d in range(self.n_sy)])

        @pl.loop(1, self.n_sx)
        def _(d):
            mine = self.whole.at[self.sx]
            self.send(2, mine, mine, (lax.rem(self.sx + d, self.n_sx), self.sy))

    def result(self):
        self.arrived(2)
        return self.whole[...].reshape(-1, 128)

    def finish(self):
        for round_, span in enumerate(self.spans()):
            pltpu.make_async_copy(span, span, self.send_sem.at[round_]).wait()


def basis_kernel(n_sx, n_sy, start_hbm, blocks_hbm, near_hbm, lists_hbm, high_hbm, low_hbm, upper_ref, inverse_ref,
                 near_ref, lists_ref, start_vm, stage, tiles, ext_a, ext_b, high, low, send, recv,
                 local_1, chunks_1, planes_1, whole_1, local_2, chunks_2, planes_2, whole_2,
                 index_sem, start_sem, block_sem, out_sem, send_sem, recv_sem, sum_send_1, sum_recv_1, sum_send_2, sum_recv_2):
    sx, sy = lax.axis_index("sx"), lax.axis_index("sy")
    count_rhs, rows = start_hbm.shape
    pairs = rows // 128
    groups = block_sem.shape[0]
    width = rows // groups
    per_group = width // 128
    sum_1 = SumOverDevices((n_sx, n_sy), (sx, sy), (local_1, chunks_1, planes_1, whole_1), sum_send_1, sum_recv_1)
    sum_2 = SumOverDevices((n_sx, n_sy), (sx, sy), (local_2, chunks_2, planes_2, whole_2), sum_send_2, sum_recv_2)

    near_copy = pltpu.make_async_copy(near_hbm, near_ref, index_sem.at[0])
    lists_copy = pltpu.make_async_copy(lists_hbm, lists_ref, index_sem.at[1])
    start_copy = pltpu.make_async_copy(start_hbm, start_vm, start_sem)
    start_copy.start()
    lists_copy.start()
    near_copy.start()
    block_copies = []
    for c in range(groups):
        copy = pltpu.make_async_copy(blocks_hbm.at[:, :, pl.ds(c * width, width)], stage.at[:, :, pl.ds(c * width, width)], block_sem.at[c])
        copy.start()
        block_copies.append(copy)

    barrier = pltpu.get_barrier_semaphore()

    @pl.loop(1, n_sx)
    def _(d):
        pl.semaphore_signal(barrier, inc=1, device_id=(lax.rem(sx + d, n_sx), sy), device_id_type=MESH)

    @pl.loop(1, n_sy)
    def _(d):
        pl.semaphore_signal(barrier, inc=1, device_id=(sx, lax.rem(sy + d, n_sy)), device_id_type=MESH)

    left_half = lax.broadcasted_iota(jnp.int32, (count_rhs, 128), 1) < 64

    def spread(pair, ext, slot):
        turned = pltpu.roll(pair, 64, 1)
        for side, both in enumerate((jnp.where(left_half, pair, turned), jnp.where(left_half, turned, pair))):
            h, l = split(both)
            ext[slot + side, 0] = h
            ext[slot + side, 1] = l

    def keep(pair, p, power):
        h, l = split(pair)
        at = pl.ds(pl.multiple_of(p * 128, 128), 128)
        high[power * count_rhs:(power + 1) * count_rhs, at] = h
        low[power * count_rhs:(power + 1) * count_rhs, at] = l

    def exchange(ext, turn):
        targets = (
            (lax.rem(sx + 1, n_sx), sy),
            (lax.rem(sx + n_sx - 1, n_sx), sy),
            (sx, lax.rem(sy + 1, n_sy)),
            (sx, lax.rem(sy + n_sy - 1, n_sy)),
        )
        copies = {}
        for d in (2, 3, 0, 1):
            for g in range(4):
                first, second = lists_ref[0, 0, d, 2 * g], lists_ref[0, 0, d, 2 * g + 1]
                one = ext[first, 0].astype(F32) + ext[first, 1].astype(F32)
                two = ext[second, 0].astype(F32) + ext[second, 1].astype(F32)
                send[turn, d, g] = jnp.where(left_half, one, two)
            if turn == 0 and d == 2:
                pl.semaphore_wait(barrier, n_sx + n_sy - 2)
            copy = pltpu.make_async_remote_copy(
                src_ref=send.at[turn, d], dst_ref=recv.at[turn, d],
                send_sem=send_sem.at[turn, d], recv_sem=recv_sem.at[turn, d],
                device_id=targets[d], device_id_type=MESH)
            copy.start()
            copies[d] = copy
        return copies

    def arrive(copies, ext, turn):
        for d in range(4):
            copies[d].wait()
            for g in range(4):
                spread(recv[turn, d, g], ext, 64 + d * 8 + 2 * g)

    def power(ext, use):
        @pl.loop(0, pairs, unroll=8)
        def _(p):
            lhs = []
            for hl in range(2):
                for side in range(2):
                    e = 2 * p + side
                    slots = [e] + [near_ref[k, e] for k in range(6)] + [near_ref[5, e]]
                    lhs.append(jnp.concatenate(
                        [jnp.where(left_half, ext[slots[2 * k], hl], ext[slots[2 * k + 1], hl]) for k in range(4)], axis=1))
            out = jnp.dot(jnp.concatenate(lhs, axis=0), tiles[p], preferred_element_type=F32)
            out = out[:, :128] + out[:, 128:]
            out = out[:2 * count_rhs] + out[2 * count_rhs:]
            use(p, jnp.where(left_half, out[:count_rhs], out[count_rhs:]))

    start_copy.wait()

    @pl.loop(0, pairs, unroll=4)
    def _(p):
        pair = start_vm[:, pl.ds(pl.multiple_of(p * 128, 128), 128)]
        keep(pair, p, 0)
        spread(pair, ext_a, 2 * p)

    lists_copy.wait()
    near_copy.wait()
    copies = exchange(ext_a, 0)

    for c in range(groups):
        block_copies[c].wait()

        @pl.loop(c * per_group, (c + 1) * per_group)
        def _(p):
            at = pl.ds(pl.multiple_of(p * 128, 128), 128)
            for k in range(7):
                h, l = split(stage[k, :, at])
                tiles[p, k * 64:(k + 1) * 64, 0:128] = h
                tiles[p, k * 64:(k + 1) * 64, 128:256] = l
            tiles[p, 448:512, :] = jnp.zeros((64, 256), BF16)

    arrive(copies, ext_a, 0)

    def first(p, pair):
        keep(pair, p, 1)
        spread(pair, ext_b, 2 * p)

    power(ext_a, first)
    copies = exchange(ext_b, 1)

    depth = 1024
    dims = (((1,), (1,)), ((), ()))

    def products_1(c, total):
        at = pl.ds(pl.multiple_of(c * depth, depth), depth)
        h, l = high[0:2 * count_rhs, at], low[0:2 * count_rhs, at]
        return total + lax.dot_general(h, jnp.concatenate([h, l], axis=0), dims, preferred_element_type=F32)

    total = lax.fori_loop(0, rows // depth, products_1, jnp.zeros((128, 256), F32))
    sum_1.scatter(total[:, :128] + total[:, 128:] + total[:, 128:].T)

    arrive(copies, ext_b, 1)
    sum_1.exchange()
    power(ext_b, lambda p, pair: keep(pair, p, 2))
    sum_1.gather()

    def products_2(c, totals):
        at = pl.ds(pl.multiple_of(c * depth, depth), depth)
        new = jnp.concatenate([high[128:192, at], low[128:192, at]], axis=0)
        old = jnp.concatenate([high[0:128, at], low[0:128, at]], axis=0)
        return (totals[0] + lax.dot_general(new, old, dims, preferred_element_type=F32),
                totals[1] + lax.dot_general(new, new, dims, preferred_element_type=F32))

    across, corner = lax.fori_loop(0, rows // depth, products_2, (jnp.zeros((128, 256), F32), jnp.zeros((128, 128), F32)))
    across = across[:64, :128] + across[:64, 128:] + across[64:, :128]
    corner = corner[:64, :64] + corner[:64, 64:] + corner[64:, :64]
    sum_2.scatter(jnp.concatenate([across, jnp.concatenate([corner, jnp.zeros((64, 64), F32)], axis=1)], axis=0))

    out_copies = [pltpu.make_async_copy(high, high_hbm, out_sem.at[0]), pltpu.make_async_copy(low, low_hbm, out_sem.at[1])]
    for copy in out_copies:
        copy.start()

    none = jnp.zeros((64, 64), F32)
    full = sum_1.result()
    u00, x00 = factor(full[0:64, 0:64])
    u01 = exact_dot(x00, full[0:64, 64:128], (1, 0))
    s11 = full[64:128, 64:128] - exact_dot(u01, u01, (0, 0))
    sum_2.exchange()
    u11, x11 = factor(s11)
    sum_2.gather()
    x10 = -exact_dot(x11, exact_dot(u01, x00, (0, 0)), (1, 0))
    x1 = jnp.concatenate([jnp.concatenate([x00, none], axis=1), jnp.concatenate([x10, x11], axis=1)], axis=0)
    upper_ref[0:64, 0:128] = jnp.concatenate([u00, u01], axis=1)
    upper_ref[64:128, 0:128] = jnp.concatenate([none, u11], axis=1)
    upper_ref[128:192, 0:128] = jnp.zeros((64, 128), F32)
    inverse_ref[0:128, 0:128] = x1
    inverse_ref[0:128, 128:192] = jnp.zeros((128, 64), F32)

    full = sum_2.result()
    u2 = exact_dot(x1, full[0:64], (1, 1))
    u22, x22 = factor(full[64:128, 0:64] - exact_dot(u2, u2, (0, 0)))
    inverse_ref[128:192, 0:128] = -exact_dot(x22, exact_dot(u2, x1, (0, 0)), (1, 0))
    inverse_ref[128:192, 128:192] = x22
    upper_ref[0:128, 128:192] = u2
    upper_ref[128:192, 128:192] = u22

    for copy in out_copies:
        copy.wait()
    sum_1.finish()
    sum_2.finish()


def result_kernel(scale, high_ref, low_ref, upper_ref, inverse_ref, q_ref, r_ref):
    xh, xl = split(inverse_ref[...] * scale)
    both = jnp.concatenate([xh, xl], axis=0)
    size = xh.shape[0]
    out = jnp.dot(both, high_ref[...], preferred_element_type=F32)
    q_ref[...] = out[:size] + out[size:] + jnp.dot(xh, low_ref[...], preferred_element_type=F32)
    r_ref[...] = upper_ref[...] / scale


def shards(n_sx, n_sy, start_block, blocks, neighbors, ghost_lists):
    count_rhs, rows = start_block.shape
    size = 3 * count_rhs
    pairs = rows // 128
    per = 128 // n_sx
    groups = 8
    sum_buffers = [pltpu.VMEM((count, per, 128), F32) for count in (n_sx, n_sx - 1, n_sy, n_sx)]
    anywhere = pl.BlockSpec(memory_space=pl.ANY)
    in_hbm = pl.BlockSpec(memory_space=pltpu.HBM)
    vmem = pl.BlockSpec(memory_space=pltpu.VMEM)
    high, low, upper, inverse = pl.pallas_call(
        functools.partial(basis_kernel, n_sx, n_sy),
        out_shape=(
            jax.ShapeDtypeStruct((size, rows), BF16),
            jax.ShapeDtypeStruct((size, rows), BF16),
            jax.ShapeDtypeStruct((size, size), F32),
            jax.ShapeDtypeStruct((size, size), F32),
        ),
        in_specs=[in_hbm, in_hbm, in_hbm, in_hbm],
        out_specs=(anywhere, anywhere, vmem, vmem),
        scratch_shapes=[
            pltpu.SMEM(neighbors.shape, jnp.int32),
            pltpu.SMEM(ghost_lists.shape, jnp.int32),
            pltpu.VMEM((count_rhs, rows), F32),
            pltpu.VMEM((7, 64, rows), F32),
            pltpu.VMEM((pairs, 512, 256), BF16),
            pltpu.VMEM((96, 2, count_rhs, 128), BF16),
            pltpu.VMEM((96, 2, count_rhs, 128), BF16),
            pltpu.VMEM((size, rows), BF16),
            pltpu.VMEM((size, rows), BF16),
            pltpu.VMEM((2, 4, 4, count_rhs, 128), F32),
            pltpu.VMEM((2, 4, 4, count_rhs, 128), F32),
            *sum_buffers,
            *sum_buffers,
            pltpu.SemaphoreType.DMA((2,)),
            pltpu.SemaphoreType.DMA,
            pltpu.SemaphoreType.DMA((groups,)),
            pltpu.SemaphoreType.DMA((2,)),
            pltpu.SemaphoreType.DMA((2, 4)),
            pltpu.SemaphoreType.DMA((2, 4)),
            *[pltpu.SemaphoreType.DMA((3,))] * 4,
        ],
        compiler_params=pltpu.CompilerParams(
            collective_id=0, has_side_effects=True, vmem_limit_bytes=56 * 1024 * 1024),
        name="basis_and_factor",
    )(start_block, blocks, neighbors, ghost_lists)

    scale = math.sqrt(rows * n_sx * n_sy)
    tile = 1024
    return pl.pallas_call(
        functools.partial(result_kernel, scale),
        grid=(rows // tile,),
        out_shape=(jax.ShapeDtypeStruct((size, rows), F32), jax.ShapeDtypeStruct((size, size), F32)),
        in_specs=[
            pl.BlockSpec((size, tile), lambda i: (0, i)),
            pl.BlockSpec((size, tile), lambda i: (0, i)),
            pl.BlockSpec((size, size), lambda i: (0, 0)),
            pl.BlockSpec((size, size), lambda i: (0, 0)),
        ],
        out_specs=(pl.BlockSpec((size, tile), lambda i: (0, i)), pl.BlockSpec((size, size), lambda i: (0, 0))),
        compiler_params=pltpu.CompilerParams(vmem_limit_bytes=56 * 1024 * 1024),
        name="orthonormal_rows",
    )(high, low, upper, inverse)


def solution(mesh):
    return jax.shard_map(
        functools.partial(shards, mesh.shape["sx"], mesh.shape["sy"]),
        mesh=mesh,
        in_specs=(
            P(None, ("sx", "sy")),
            P(None, None, ("sx", "sy")),
            P(None, ("sx", "sy")),
            P("sx", "sy", None, None),
        ),
        out_specs=(P(None, ("sx", "sy")), P()),
        check_vma=False,
    )
```

```python
import functools
import math

import jax
import jax.numpy as jnp
from jax import lax
from jax.experimental import pallas as pl
from jax.experimental.pallas import tpu as pltpu
from jax.sharding import PartitionSpec as P

MESH = pl.DeviceIdType.MESH
F32 = jnp.float32
BF16 = jnp.bfloat16
HIGHEST = lax.Precision.HIGHEST


def split(value):
    high = value.astype(BF16)
    low = (value - high.astype(F32)).astype(BF16)
    return high, low


def exact_dot(a, b, contract):
    return lax.dot_general(a, b, ((contract[0:1], contract[1:2]), ((), ())), precision=HIGHEST, preferred_element_type=F32)


def factor(matrix):
    size = matrix.shape[0]
    shape = (8, 2 * size)
    count = size // 8
    rows = lax.broadcasted_iota(jnp.int32, (size, size), 0)
    cols = lax.broadcasted_iota(jnp.int32, (size, size), 1)
    wide = jnp.concatenate([matrix, jnp.where(rows == cols, 1.0, 0.0).astype(F32)], axis=1)
    parts = [wide[8 * b:8 * b + 8] for b in range(count)]
    sub = lax.broadcasted_iota(jnp.int32, shape, 0)
    lane = lax.broadcasted_iota(jnp.int32, shape, 1)
    done = []
    for t in range(count):
        spread_cols = [[jnp.broadcast_to(parts[b][:, 8 * t + k:8 * t + k + 1], shape) for b in range(t, count)] for k in range(8)]
        spread_rows = [jnp.broadcast_to(parts[t][i:i + 1], shape) for i in range(8)]
        entry = [[jnp.broadcast_to(spread_cols[k][0][i:i + 1], shape) for k in range(i + 1)] for i in range(8)]
        inverse = []
        for j in range(8):
            inverse.append(1.0 / entry[j][j])
            ratio = [None] * 8
            for i in range(j + 1, 8):
                ratio[i] = entry[i][j] * inverse[j]
                for k in range(j + 1, i + 1):
                    entry[i][k] = entry[i][k] - ratio[i] * entry[k][j]
                spread_rows[i] = spread_rows[i] - ratio[i] * spread_rows[j]
                for b in range(1, count - t):
                    spread_cols[i][b] = spread_cols[i][b] - ratio[i] * spread_cols[j][b]
            scaled = spread_rows[j] * inverse[j]
            for b in range(1, count - t):
                parts[t + b] = parts[t + b] - spread_cols[j][b] * scaled
        own = spread_rows[0] / jnp.sqrt(entry[0][0])
        for i in range(1, 8):
            own = jnp.where(sub == i, spread_rows[i] / jnp.sqrt(entry[i][i]), own)
        done.append(jnp.where(lane < sub + 8 * t, 0.0, own))
    result = jnp.concatenate(done, axis=0)
    return result[:, :size], result[:, size:]


def add_up(parts):
    while len(parts) > 1:
        parts = [parts[i] + parts[i + 1] if i + 1 < len(parts) else parts[i] for i in range(0, len(parts), 2)]
    return parts[0]


def ring_hops(d, n):
    return min(d, n - d)


def others_along(sx, sy, n_sx, n_sy):
    n_x = 4 if n_sx == 32 else 1
    n_y = n_sx // (2 * n_x)
    x, y, core = sx // (2 * n_y), (sx // 2) % n_y, sx % 2
    steps = [(dx, dy, dc) for dx in range(n_x) for dy in range(n_y) for dc in range(2)][1:]
    steps.sort(key=lambda step: -(2 * ring_hops(step[0], n_x) + 2 * ring_hops(step[1], n_y) + step[2]))
    along_x = [((lax.rem(x + dx, n_x) * n_y + lax.rem(y + dy, n_y)) * 2 + lax.rem(core + dc, 2)) for dx, dy, dc in steps]
    along_y = [lax.rem(sy + d, n_sy) for d in sorted(range(1, n_sy), key=lambda d: -ring_hops(d, n_sy))]
    return along_x, along_y


class SumOverDevices:
    def __init__(self, shape, place, others, refs, send_sem, recv_sem):
        self.n_sx, self.n_sy = shape
        self.sx, self.sy = place
        self.others_x, self.others_y = others
        self.local, self.chunks, self.planes, self.whole = refs
        self.send_sem, self.recv_sem = send_sem, recv_sem

    def send(self, round_, source, target, device):
        pltpu.make_async_remote_copy(
            src_ref=source, dst_ref=target, send_sem=self.send_sem.at[round_], recv_sem=self.recv_sem.at[round_],
            device_id=device, device_id_type=MESH).start()

    def spans(self):
        return (self.chunks, self.planes.at[pl.ds(0, self.n_sy - 1)], self.whole.at[pl.ds(0, self.n_sx - 1)])

    def arrived(self, round_):
        span = self.spans()[round_]
        pltpu.make_async_copy(span, span, self.recv_sem.at[round_]).wait()

    def scatter(self, value):
        self.local[...] = value.reshape(self.local.shape)

        for slot, other in enumerate(self.others_x):
            self.send(0, self.local.at[other], self.chunks.at[slot], (other, self.sy))

    def exchange(self):
        self.arrived(0)
        self.planes[self.sy] = add_up([self.local[self.sx]] + [self.chunks[d] for d in range(self.n_sx - 1)])

        mine = self.planes.at[self.sy]
        for other in self.others_y:
            self.send(1, mine, mine, (self.sx, other))

    def gather(self):
        self.arrived(1)
        self.whole[self.sx] = add_up([self.planes[d] for d in range(self.n_sy)])

        mine = self.whole.at[self.sx]
        for other in self.others_x:
            self.send(2, mine, mine, (other, self.sy))

    def result(self):
        self.arrived(2)
        return self.whole[...].reshape(-1, 128)

    def finish(self):
        for round_, span in enumerate(self.spans()):
            pltpu.make_async_copy(span, span, self.send_sem.at[round_]).wait()


def basis_kernel(n_sx, n_sy, start_hbm, blocks_hbm, near_hbm, lists_hbm, high_hbm, low_hbm, upper_ref, inverse_ref,
                 near_ref, lists_ref, start_vm, stage, tiles, ext_a, ext_b, high, low, send, recv,
                 local_1, chunks_1, planes_1, whole_1, local_2, chunks_2, planes_2, whole_2,
                 index_sem, start_sem, block_sem, out_sem, send_sem, recv_sem, sum_send_1, sum_recv_1, sum_send_2, sum_recv_2):
    sx, sy = lax.axis_index("sx"), lax.axis_index("sy")
    count_rhs, rows = start_hbm.shape
    pairs = rows // 128
    groups = block_sem.shape[0]
    width = rows // groups
    per_group = width // 128
    others = others_along(sx, sy, n_sx, n_sy)
    sum_1 = SumOverDevices((n_sx, n_sy), (sx, sy), others, (local_1, chunks_1, planes_1, whole_1), sum_send_1, sum_recv_1)
    sum_2 = SumOverDevices((n_sx, n_sy), (sx, sy), others, (local_2, chunks_2, planes_2, whole_2), sum_send_2, sum_recv_2)

    near_copy = pltpu.make_async_copy(near_hbm, near_ref, index_sem.at[0])
    lists_copy = pltpu.make_async_copy(lists_hbm, lists_ref, index_sem.at[1])
    start_copy = pltpu.make_async_copy(start_hbm, start_vm, start_sem)
    start_copy.start()
    lists_copy.start()
    near_copy.start()
    block_copies = []
    for c in range(groups):
        copy = pltpu.make_async_copy(blocks_hbm.at[:, :, pl.ds(c * width, width)], stage.at[:, :, pl.ds(c * width, width)], block_sem.at[c])
        copy.start()
        block_copies.append(copy)

    barrier = pltpu.get_barrier_semaphore()

    @pl.loop(1, n_sx)
    def _(d):
        pl.semaphore_signal(barrier, inc=1, device_id=(lax.rem(sx + d, n_sx), sy), device_id_type=MESH)

    @pl.loop(1, n_sy)
    def _(d):
        pl.semaphore_signal(barrier, inc=1, device_id=(sx, lax.rem(sy + d, n_sy)), device_id_type=MESH)

    left_half = lax.broadcasted_iota(jnp.int32, (count_rhs, 128), 1) < 64

    def spread(pair, ext, slot):
        turned = pltpu.roll(pair, 64, 1)
        for side, both in enumerate((jnp.where(left_half, pair, turned), jnp.where(left_half, turned, pair))):
            h, l = split(both)
            ext[slot + side, 0] = h
            ext[slot + side, 1] = l

    def keep(pair, p, power):
        h, l = split(pair)
        at = pl.ds(pl.multiple_of(p * 128, 128), 128)
        high[power * count_rhs:(power + 1) * count_rhs, at] = h
        low[power * count_rhs:(power + 1) * count_rhs, at] = l

    def exchange(ext, turn):
        targets = (
            (lax.rem(sx + 1, n_sx), sy),
            (lax.rem(sx + n_sx - 1, n_sx), sy),
            (sx, lax.rem(sy + 1, n_sy)),
            (sx, lax.rem(sy + n_sy - 1, n_sy)),
        )
        copies = {}
        for d in (2, 3, 0, 1):
            for g in range(4):
                first, second = lists_ref[0, 0, d, 2 * g], lists_ref[0, 0, d, 2 * g + 1]
                one = ext[first, 0].astype(F32) + ext[first, 1].astype(F32)
                two = ext[second, 0].astype(F32) + ext[second, 1].astype(F32)
                send[turn, d, g] = jnp.where(left_half, one, two)
            if turn == 0 and d == 2:
                pl.semaphore_wait(barrier, n_sx + n_sy - 2)
            copy = pltpu.make_async_remote_copy(
                src_ref=send.at[turn, d], dst_ref=recv.at[turn, d],
                send_sem=send_sem.at[turn, d], recv_sem=recv_sem.at[turn, d],
                device_id=targets[d], device_id_type=MESH)
            copy.start()
            copies[d] = copy
        return copies

    def arrive(copies, ext, turn):
        for d in range(4):
            copies[d].wait()
            for g in range(4):
                spread(recv[turn, d, g], ext, 64 + d * 8 + 2 * g)

    def power(ext, use):
        @pl.loop(0, pairs, unroll=16)
        def _(p):
            lhs = []
            for hl in range(2):
                for side in range(2):
                    e = 2 * p + side
                    slots = [e] + [near_ref[k, e] for k in range(6)] + [near_ref[5, e]]
                    lhs.append(jnp.concatenate(
                        [jnp.where(left_half, ext[slots[2 * k], hl], ext[slots[2 * k + 1], hl]) for k in range(4)], axis=1))
            out = jnp.dot(jnp.concatenate(lhs, axis=0), tiles[p], preferred_element_type=F32)
            out = out[:, :128] + out[:, 128:]
            out = out[:2 * count_rhs] + out[2 * count_rhs:]
            use(p, jnp.where(left_half, out[:count_rhs], out[count_rhs:]))

    start_copy.wait()

    @pl.loop(0, pairs, unroll=4)
    def _(p):
        pair = start_vm[:, pl.ds(pl.multiple_of(p * 128, 128), 128)]
        keep(pair, p, 0)
        spread(pair, ext_a, 2 * p)

    lists_copy.wait()
    near_copy.wait()
    copies = exchange(ext_a, 0)

    for c in range(groups):
        block_copies[c].wait()

        @pl.loop(c * per_group, (c + 1) * per_group)
        def _(p):
            at = pl.ds(pl.multiple_of(p * 128, 128), 128)
            for k in range(7):
                h, l = split(stage[k, :, at])
                tiles[p, k * 64:(k + 1) * 64, 0:128] = h
                tiles[p, k * 64:(k + 1) * 64, 128:256] = l
            tiles[p, 448:512, :] = jnp.zeros((64, 256), BF16)

    arrive(copies, ext_a, 0)

    def first(p, pair):
        keep(pair, p, 1)
        spread(pair, ext_b, 2 * p)

    power(ext_a, first)
    copies = exchange(ext_b, 1)

    depth = 1024
    dims = (((1,), (1,)), ((), ()))

    def products_1(c, total):
        at = pl.ds(pl.multiple_of(c * depth, depth), depth)
        h, l = high[0:2 * count_rhs, at], low[0:2 * count_rhs, at]
        return total + lax.dot_general(h, jnp.concatenate([h, l], axis=0), dims, preferred_element_type=F32)

    total = lax.fori_loop(0, rows // depth, products_1, jnp.zeros((128, 256), F32))
    sum_1.scatter(total[:, :128] + total[:, 128:] + total[:, 128:].T)

    arrive(copies, ext_b, 1)
    sum_1.exchange()
    power(ext_b, lambda p, pair: keep(pair, p, 2))

    def products_2(c, totals):
        at = pl.ds(pl.multiple_of(c * depth, depth), depth)
        new = jnp.concatenate([high[128:192, at], low[128:192, at]], axis=0)
        old = jnp.concatenate([high[0:128, at], low[0:128, at]], axis=0)
        return (totals[0] + lax.dot_general(new, old, dims, preferred_element_type=F32),
                totals[1] + lax.dot_general(new, new, dims, preferred_element_type=F32))

    across, corner = lax.fori_loop(0, rows // depth, products_2, (jnp.zeros((128, 256), F32), jnp.zeros((128, 128), F32)))
    across = across[:64, :128] + across[:64, 128:] + across[64:, :128]
    corner = corner[:64, :64] + corner[:64, 64:] + corner[64:, :64]
    sum_2.scatter(jnp.concatenate([across, jnp.concatenate([corner, jnp.zeros((64, 64), F32)], axis=1)], axis=0))

    out_copies = [pltpu.make_async_copy(high, high_hbm, out_sem.at[0]), pltpu.make_async_copy(low, low_hbm, out_sem.at[1])]
    for copy in out_copies:
        copy.start()

    sum_1.gather()
    sum_2.exchange()
    none = jnp.zeros((64, 64), F32)
    full = sum_1.result()
    u00, x00 = factor(full[0:64, 0:64])
    u01 = exact_dot(x00, full[0:64, 64:128], (1, 0))
    s11 = full[64:128, 64:128] - exact_dot(u01, u01, (0, 0))
    sum_2.gather()
    u11, x11 = factor(s11)
    x10 = -exact_dot(x11, exact_dot(u01, x00, (0, 0)), (1, 0))
    x1 = jnp.concatenate([jnp.concatenate([x00, none], axis=1), jnp.concatenate([x10, x11], axis=1)], axis=0)
    upper_ref[0:64, 0:128] = jnp.concatenate([u00, u01], axis=1)
    upper_ref[64:128, 0:128] = jnp.concatenate([none, u11], axis=1)
    upper_ref[128:192, 0:128] = jnp.zeros((64, 128), F32)
    inverse_ref[0:128, 0:128] = x1
    inverse_ref[0:128, 128:192] = jnp.zeros((128, 64), F32)

    full = sum_2.result()
    u2 = exact_dot(x1, full[0:64], (1, 1))
    u22, x22 = factor(full[64:128, 0:64] - exact_dot(u2, u2, (0, 0)))
    inverse_ref[128:192, 0:128] = -exact_dot(x22, exact_dot(u2, x1, (0, 0)), (1, 0))
    inverse_ref[128:192, 128:192] = x22
    upper_ref[0:128, 128:192] = u2
    upper_ref[128:192, 128:192] = u22

    for copy in out_copies:
        copy.wait()
    sum_1.finish()
    sum_2.finish()


def result_kernel(scale, high_hbm, low_hbm, upper_hbm, inverse_hbm, q_hbm, r_hbm, high, low, q, upper, inverse, r, in_sem, out_sem, small_sem):
    chunks = out_sem.shape[0]
    width = q.shape[1] // chunks
    loads, stores = [], []
    for c in range(chunks):
        at = pl.ds(c * width, width)
        loads.append((pltpu.make_async_copy(high_hbm.at[:, at], high.at[:, at], in_sem.at[0, c]),
                      pltpu.make_async_copy(low_hbm.at[:, at], low.at[:, at], in_sem.at[1, c])))
        stores.append(pltpu.make_async_copy(q.at[:, at], q_hbm.at[:, at], out_sem.at[c]))
    small = [pltpu.make_async_copy(inverse_hbm, inverse, small_sem.at[0]), pltpu.make_async_copy(upper_hbm, upper, small_sem.at[1])]
    small[0].start()
    for pair in loads:
        for copy in pair:
            copy.start()
    small[1].start()
    small[0].wait()
    xh, xl = split(inverse[...] * scale)
    left = jnp.concatenate([xh, xh, xl], axis=1)
    for c in range(chunks):
        for copy in loads[c]:
            copy.wait()
        at = pl.ds(c * width, width)
        h = high[:, at]
        q[:, at] = jnp.dot(left, jnp.concatenate([h, low[:, at], h], axis=0), preferred_element_type=F32)
        stores[c].start()
        if c == 0:
            small[1].wait()
            r[...] = upper[...] / scale
            stores.append(pltpu.make_async_copy(r, r_hbm, small_sem.at[2]))
            stores[-1].start()
    for store in stores:
        store.wait()


def shards(n_sx, n_sy, start_block, blocks, neighbors, ghost_lists):
    count_rhs, rows = start_block.shape
    size = 3 * count_rhs
    pairs = rows // 128
    per = 128 // n_sx
    groups = 8
    sum_buffers = [pltpu.VMEM((count, per, 128), F32) for count in (n_sx, n_sx - 1, n_sy, n_sx)]
    anywhere = pl.BlockSpec(memory_space=pl.ANY)
    in_hbm = pl.BlockSpec(memory_space=pltpu.HBM)
    vmem = pl.BlockSpec(memory_space=pltpu.VMEM)
    high, low, upper, inverse = pl.pallas_call(
        functools.partial(basis_kernel, n_sx, n_sy),
        out_shape=(
            jax.ShapeDtypeStruct((size, rows), BF16),
            jax.ShapeDtypeStruct((size, rows), BF16),
            jax.ShapeDtypeStruct((size, size), F32),
            jax.ShapeDtypeStruct((size, size), F32),
        ),
        in_specs=[in_hbm, in_hbm, in_hbm, in_hbm],
        out_specs=(anywhere, anywhere, vmem, vmem),
        scratch_shapes=[
            pltpu.SMEM(neighbors.shape, jnp.int32),
            pltpu.SMEM(ghost_lists.shape, jnp.int32),
            pltpu.VMEM((count_rhs, rows), F32),
            pltpu.VMEM((7, 64, rows), F32),
            pltpu.VMEM((pairs, 512, 256), BF16),
            pltpu.VMEM((96, 2, count_rhs, 128), BF16),
            pltpu.VMEM((96, 2, count_rhs, 128), BF16),
            pltpu.VMEM((size, rows), BF16),
            pltpu.VMEM((size, rows), BF16),
            pltpu.VMEM((2, 4, 4, count_rhs, 128), F32),
            pltpu.VMEM((2, 4, 4, count_rhs, 128), F32),
            *sum_buffers,
            *sum_buffers,
            pltpu.SemaphoreType.DMA((2,)),
            pltpu.SemaphoreType.DMA,
            pltpu.SemaphoreType.DMA((groups,)),
            pltpu.SemaphoreType.DMA((2,)),
            pltpu.SemaphoreType.DMA((2, 4)),
            pltpu.SemaphoreType.DMA((2, 4)),
            *[pltpu.SemaphoreType.DMA((3,))] * 4,
        ],
        compiler_params=pltpu.CompilerParams(
            collective_id=0, has_side_effects=True, vmem_limit_bytes=56 * 1024 * 1024),
        name="basis_and_factor",
    )(start_block, blocks, neighbors, ghost_lists)

    scale = math.sqrt(rows * n_sx * n_sy)
    parts = 4
    return pl.pallas_call(
        functools.partial(result_kernel, scale),
        out_shape=(jax.ShapeDtypeStruct((size, rows), F32), jax.ShapeDtypeStruct((size, size), F32)),
        in_specs=[anywhere] * 4,
        out_specs=(anywhere, anywhere),
        scratch_shapes=[
            pltpu.VMEM((size, rows), BF16),
            pltpu.VMEM((size, rows), BF16),
            pltpu.VMEM((size, rows), F32),
            pltpu.VMEM((size, size), F32),
            pltpu.VMEM((size, size), F32),
            pltpu.VMEM((size, size), F32),
            pltpu.SemaphoreType.DMA((2, parts)),
            pltpu.SemaphoreType.DMA((parts,)),
            pltpu.SemaphoreType.DMA((3,)),
        ],
        compiler_params=pltpu.CompilerParams(vmem_limit_bytes=56 * 1024 * 1024),
        name="orthonormal_rows",
    )(high, low, upper, inverse)


def solution(mesh):
    return jax.shard_map(
        functools.partial(shards, mesh.shape["sx"], mesh.shape["sy"]),
        mesh=mesh,
        in_specs=(
            P(None, ("sx", "sy")),
            P(None, None, ("sx", "sy")),
            P(None, ("sx", "sy")),
            P("sx", "sy", None, None),
        ),
        out_specs=(P(None, ("sx", "sy")), P()),
        check_vma=False,
    )
```

```python
import functools
import math

import jax
import jax.numpy as jnp
from jax import lax
from jax.experimental import pallas as pl
from jax.experimental.pallas import tpu as pltpu
from jax.sharding import PartitionSpec as P

MESH = pl.DeviceIdType.MESH
F32 = jnp.float32
BF16 = jnp.bfloat16
HIGHEST = lax.Precision.HIGHEST


def split(value):
    high = value.astype(BF16)
    low = (value - high.astype(F32)).astype(BF16)
    return high, low


def exact_dot(a, b, contract):
    return lax.dot_general(a, b, ((contract[0:1], contract[1:2]), ((), ())), precision=HIGHEST, preferred_element_type=F32)


def factor(matrix):
    size = matrix.shape[0]
    shape = (8, 2 * size)
    count = size // 8
    rows = lax.broadcasted_iota(jnp.int32, (size, size), 0)
    cols = lax.broadcasted_iota(jnp.int32, (size, size), 1)
    wide = jnp.concatenate([matrix, jnp.where(rows == cols, 1.0, 0.0).astype(F32)], axis=1)
    parts = [wide[8 * b:8 * b + 8] for b in range(count)]
    sub = lax.broadcasted_iota(jnp.int32, shape, 0)
    lane = lax.broadcasted_iota(jnp.int32, shape, 1)
    done = []
    for t in range(count):
        spread_cols = [[jnp.broadcast_to(parts[b][:, 8 * t + k:8 * t + k + 1], shape) for b in range(t, count)] for k in range(8)]
        spread_rows = [jnp.broadcast_to(parts[t][i:i + 1], shape) for i in range(8)]
        entry = [[jnp.broadcast_to(spread_cols[k][0][i:i + 1], shape) for k in range(i + 1)] for i in range(8)]
        inverse = []
        for j in range(8):
            inverse.append(1.0 / entry[j][j])
            ratio = [None] * 8
            for i in range(j + 1, 8):
                ratio[i] = entry[i][j] * inverse[j]
                for k in range(j + 1, i + 1):
                    entry[i][k] = entry[i][k] - ratio[i] * entry[k][j]
                spread_rows[i] = spread_rows[i] - ratio[i] * spread_rows[j]
                for b in range(1, count - t):
                    spread_cols[i][b] = spread_cols[i][b] - ratio[i] * spread_cols[j][b]
            scaled = spread_rows[j] * inverse[j]
            for b in range(1, count - t):
                parts[t + b] = parts[t + b] - spread_cols[j][b] * scaled
        own = spread_rows[0] / jnp.sqrt(entry[0][0])
        for i in range(1, 8):
            own = jnp.where(sub == i, spread_rows[i] / jnp.sqrt(entry[i][i]), own)
        done.append(jnp.where(lane < sub + 8 * t, 0.0, own))
    result = jnp.concatenate(done, axis=0)
    return result[:, :size], result[:, size:]


def add_up(parts):
    while len(parts) > 1:
        parts = [parts[i] + parts[i + 1] if i + 1 < len(parts) else parts[i] for i in range(0, len(parts), 2)]
    return parts[0]


def ring_hops(d, n):
    return min(d, n - d)


def others_along(sx, sy, n_sx, n_sy):
    n_x = 4 if n_sx == 32 else 1
    n_y = n_sx // (2 * n_x)
    x, y, core = sx // (2 * n_y), (sx // 2) % n_y, sx % 2
    steps = [(dx, dy, dc) for dx in range(n_x) for dy in range(n_y) for dc in range(2)][1:]
    steps.sort(key=lambda step: -(2 * ring_hops(step[0], n_x) + 2 * ring_hops(step[1], n_y) + step[2]))
    along_x = [((lax.rem(x + dx, n_x) * n_y + lax.rem(y + dy, n_y)) * 2 + lax.rem(core + dc, 2)) for dx, dy, dc in steps]
    along_y = [lax.rem(sy + d, n_sy) for d in sorted(range(1, n_sy), key=lambda d: -ring_hops(d, n_sy))]
    return along_x, along_y


class SumOverDevices:
    def __init__(self, shape, place, others, refs, send_sem, recv_sem):
        self.n_sx, self.n_sy = shape
        self.sx, self.sy = place
        self.others_x, self.others_y = others
        self.local, self.chunks, self.planes, self.whole = refs
        self.send_sem, self.recv_sem = send_sem, recv_sem

    def send(self, round_, source, target, device):
        pltpu.make_async_remote_copy(
            src_ref=source, dst_ref=target, send_sem=self.send_sem.at[round_], recv_sem=self.recv_sem.at[round_],
            device_id=device, device_id_type=MESH).start()

    def spans(self):
        return (self.chunks, self.planes.at[pl.ds(0, self.n_sy - 1)], self.whole.at[pl.ds(0, self.n_sx - 1)])

    def arrived(self, round_):
        span = self.spans()[round_]
        pltpu.make_async_copy(span, span, self.recv_sem.at[round_]).wait()

    def scatter(self, value):
        self.local[...] = value.reshape(self.local.shape)

        for slot, other in enumerate(self.others_x):
            self.send(0, self.local.at[other], self.chunks.at[slot], (other, self.sy))

    def exchange(self):
        self.arrived(0)
        self.planes[self.sy] = add_up([self.local[self.sx]] + [self.chunks[d] for d in range(self.n_sx - 1)])

        mine = self.planes.at[self.sy]
        for other in self.others_y:
            self.send(1, mine, mine, (self.sx, other))

    def gather(self):
        self.arrived(1)
        self.whole[self.sx] = add_up([self.planes[d] for d in range(self.n_sy)])

        mine = self.whole.at[self.sx]
        for other in self.others_x:
            self.send(2, mine, mine, (other, self.sy))

    def result(self):
        self.arrived(2)
        return self.whole[...].reshape(-1, 128)

    def finish(self):
        for round_, span in enumerate(self.spans()):
            pltpu.make_async_copy(span, span, self.send_sem.at[round_]).wait()


def basis_kernel(n_sx, n_sy, start_hbm, blocks_hbm, near_hbm, lists_hbm, high_hbm, low_hbm, upper_ref, inverse_ref,
                 near_ref, lists_ref, start_vm, stage, tiles, ext_a, ext_b, high, low, send, recv,
                 local_1, chunks_1, planes_1, whole_1, local_2, chunks_2, planes_2, whole_2,
                 index_sem, start_sem, block_sem, out_sem, send_sem, recv_sem, sum_send_1, sum_recv_1, sum_send_2, sum_recv_2):
    sx, sy = lax.axis_index("sx"), lax.axis_index("sy")
    count_rhs, rows = start_hbm.shape
    pairs = rows // 128
    groups = block_sem.shape[0]
    width = rows // groups
    per_group = width // 128
    others = others_along(sx, sy, n_sx, n_sy)
    sum_1 = SumOverDevices((n_sx, n_sy), (sx, sy), others, (local_1, chunks_1, planes_1, whole_1), sum_send_1, sum_recv_1)
    sum_2 = SumOverDevices((n_sx, n_sy), (sx, sy), others, (local_2, chunks_2, planes_2, whole_2), sum_send_2, sum_recv_2)

    near_copy = pltpu.make_async_copy(near_hbm, near_ref, index_sem.at[0])
    lists_copy = pltpu.make_async_copy(lists_hbm, lists_ref, index_sem.at[1])
    start_groups = start_sem.shape[0]
    start_width = rows // start_groups
    start_copies = []
    for c in range(start_groups):
        at = pl.ds(c * start_width, start_width)
        copy = pltpu.make_async_copy(start_hbm.at[:, at], start_vm.at[:, at], start_sem.at[c])
        copy.start()
        start_copies.append(copy)
    lists_copy.start()
    near_copy.start()
    block_copies = []
    for c in range(groups):
        copy = pltpu.make_async_copy(blocks_hbm.at[:, :, pl.ds(c * width, width)], stage.at[:, :, pl.ds(c * width, width)], block_sem.at[c])
        copy.start()
        block_copies.append(copy)

    barrier = pltpu.get_barrier_semaphore()

    @pl.loop(1, n_sx)
    def _(d):
        pl.semaphore_signal(barrier, inc=1, device_id=(lax.rem(sx + d, n_sx), sy), device_id_type=MESH)

    @pl.loop(1, n_sy)
    def _(d):
        pl.semaphore_signal(barrier, inc=1, device_id=(sx, lax.rem(sy + d, n_sy)), device_id_type=MESH)

    left_half = lax.broadcasted_iota(jnp.int32, (count_rhs, 128), 1) < 64

    def spread(pair, ext, slot):
        turned = pltpu.roll(pair, 64, 1)
        for side, both in enumerate((jnp.where(left_half, pair, turned), jnp.where(left_half, turned, pair))):
            h, l = split(both)
            ext[slot + side, 0] = h
            ext[slot + side, 1] = l

    def keep(pair, p, power):
        h, l = split(pair)
        at = pl.ds(pl.multiple_of(p * 128, 128), 128)
        high[power * count_rhs:(power + 1) * count_rhs, at] = h
        low[power * count_rhs:(power + 1) * count_rhs, at] = l

    def exchange(ext, turn):
        targets = (
            (lax.rem(sx + 1, n_sx), sy),
            (lax.rem(sx + n_sx - 1, n_sx), sy),
            (sx, lax.rem(sy + 1, n_sy)),
            (sx, lax.rem(sy + n_sy - 1, n_sy)),
        )
        copies = {}
        for d in (2, 3, 0, 1):
            for g in range(4):
                first, second = lists_ref[0, 0, d, 2 * g], lists_ref[0, 0, d, 2 * g + 1]
                one = ext[first, 0].astype(F32) + ext[first, 1].astype(F32)
                two = ext[second, 0].astype(F32) + ext[second, 1].astype(F32)
                send[turn, d, g] = jnp.where(left_half, one, two)
            if turn == 0 and d == 2:
                pl.semaphore_wait(barrier, n_sx + n_sy - 2)
            copy = pltpu.make_async_remote_copy(
                src_ref=send.at[turn, d], dst_ref=recv.at[turn, d],
                send_sem=send_sem.at[turn, d], recv_sem=recv_sem.at[turn, d],
                device_id=targets[d], device_id_type=MESH)
            copy.start()
            copies[d] = copy
        return copies

    def arrive(copies, ext, turn):
        for d in range(4):
            copies[d].wait()
            for g in range(4):
                spread(recv[turn, d, g], ext, 64 + d * 8 + 2 * g)

    def power(ext, use, first_pair, last_pair):
        @pl.loop(first_pair, last_pair, unroll=16)
        def _(p):
            lhs = []
            for hl in range(2):
                for side in range(2):
                    e = 2 * p + side
                    slots = [e] + [near_ref[k, e] for k in range(6)] + [near_ref[5, e]]
                    lhs.append(jnp.concatenate(
                        [jnp.where(left_half, ext[slots[2 * k], hl], ext[slots[2 * k + 1], hl]) for k in range(4)], axis=1))
            out = jnp.dot(jnp.concatenate(lhs, axis=0), tiles[p], preferred_element_type=F32)
            out = out[:, :128] + out[:, 128:]
            out = out[:2 * count_rhs] + out[2 * count_rhs:]
            use(p, jnp.where(left_half, out[:count_rhs], out[count_rhs:]))

    for c in range(start_groups):
        start_copies[c].wait()

        @pl.loop(c * start_width // 128, (c + 1) * start_width // 128, unroll=4)
        def _(p):
            pair = start_vm[:, pl.ds(pl.multiple_of(p * 128, 128), 128)]
            keep(pair, p, 0)
            spread(pair, ext_a, 2 * p)

    lists_copy.wait()
    near_copy.wait()
    copies = exchange(ext_a, 0)

    for c in range(groups):
        block_copies[c].wait()

        @pl.loop(c * per_group, (c + 1) * per_group)
        def _(p):
            at = pl.ds(pl.multiple_of(p * 128, 128), 128)
            for k in range(7):
                h, l = split(stage[k, :, at])
                tiles[p, k * 64:(k + 1) * 64, 0:128] = h
                tiles[p, k * 64:(k + 1) * 64, 128:256] = l
            tiles[p, 448:512, :] = jnp.zeros((64, 256), BF16)

    arrive(copies, ext_a, 0)

    def first(p, pair):
        keep(pair, p, 1)
        spread(pair, ext_b, 2 * p)

    power(ext_a, first, 0, pairs)
    copies = exchange(ext_b, 1)

    depth = 1024
    dims = (((1,), (1,)), ((), ()))

    def products_1(c, total):
        at = pl.ds(pl.multiple_of(c * depth, depth), depth)
        h, l = high[0:2 * count_rhs, at], low[0:2 * count_rhs, at]
        return total + lax.dot_general(h, jnp.concatenate([h, l], axis=0), dims, preferred_element_type=F32)

    total = lax.fori_loop(0, rows // depth, products_1, jnp.zeros((128, 256), F32))
    sum_1.scatter(total[:, :128] + total[:, 128:] + total[:, 128:].T)

    arrive(copies, ext_b, 1)
    power(ext_b, lambda p, pair: keep(pair, p, 2), 0, pairs // 2)
    sum_1.exchange()
    power(ext_b, lambda p, pair: keep(pair, p, 2), pairs // 2, pairs)

    def products_2(c, totals):
        at = pl.ds(pl.multiple_of(c * depth, depth), depth)
        new = jnp.concatenate([high[128:192, at], low[128:192, at]], axis=0)
        old = jnp.concatenate([high[0:128, at], low[0:128, at]], axis=0)
        return (totals[0] + lax.dot_general(new, old, dims, preferred_element_type=F32),
                totals[1] + lax.dot_general(new, new, dims, preferred_element_type=F32))

    across, corner = lax.fori_loop(0, rows // depth, products_2, (jnp.zeros((128, 256), F32), jnp.zeros((128, 128), F32)))
    across = across[:64, :128] + across[:64, 128:] + across[64:, :128]
    corner = corner[:64, :64] + corner[:64, 64:] + corner[64:, :64]
    sum_2.scatter(jnp.concatenate([across, jnp.concatenate([corner, jnp.zeros((64, 64), F32)], axis=1)], axis=0))

    out_copies = [pltpu.make_async_copy(high, high_hbm, out_sem.at[0]), pltpu.make_async_copy(low, low_hbm, out_sem.at[1])]
    for copy in out_copies:
        copy.start()

    sum_1.gather()
    sum_2.exchange()
    none = jnp.zeros((64, 64), F32)
    full = sum_1.result()
    u00, x00 = factor(full[0:64, 0:64])
    u01 = exact_dot(x00, full[0:64, 64:128], (1, 0))
    s11 = full[64:128, 64:128] - exact_dot(u01, u01, (0, 0))
    sum_2.gather()
    u11, x11 = factor(s11)
    x10 = -exact_dot(x11, exact_dot(u01, x00, (0, 0)), (1, 0))
    x1 = jnp.concatenate([jnp.concatenate([x00, none], axis=1), jnp.concatenate([x10, x11], axis=1)], axis=0)
    upper_ref[0:64, 0:128] = jnp.concatenate([u00, u01], axis=1)
    upper_ref[64:128, 0:128] = jnp.concatenate([none, u11], axis=1)
    upper_ref[128:192, 0:128] = jnp.zeros((64, 128), F32)
    inverse_ref[0:128, 0:128] = x1
    inverse_ref[0:128, 128:192] = jnp.zeros((128, 64), F32)

    full = sum_2.result()
    u2 = exact_dot(x1, full[0:64], (1, 1))
    u22, x22 = factor(full[64:128, 0:64] - exact_dot(u2, u2, (0, 0)))
    inverse_ref[128:192, 0:128] = -exact_dot(x22, exact_dot(u2, x1, (0, 0)), (1, 0))
    inverse_ref[128:192, 128:192] = x22
    upper_ref[0:128, 128:192] = u2
    upper_ref[128:192, 128:192] = u22

    for copy in out_copies:
        copy.wait()
    sum_1.finish()
    sum_2.finish()


def result_kernel(scale, spans, high_hbm, low_hbm, upper_hbm, inverse_hbm, q_hbm, r_hbm, high, low, q, upper, inverse, r, in_sem, out_sem, small_sem):
    loads, stores = [], []
    for c, at in enumerate(spans):
        at = pl.ds(*at)
        loads.append((pltpu.make_async_copy(high_hbm.at[:, at], high.at[:, at], in_sem.at[0, c]),
                      pltpu.make_async_copy(low_hbm.at[:, at], low.at[:, at], in_sem.at[1, c])))
        stores.append(pltpu.make_async_copy(q.at[:, at], q_hbm.at[:, at], out_sem.at[c]))
    small = [pltpu.make_async_copy(inverse_hbm, inverse, small_sem.at[0]), pltpu.make_async_copy(upper_hbm, upper, small_sem.at[1])]
    small[0].start()
    for pair in loads:
        for copy in pair:
            copy.start()
    small[1].start()
    small[0].wait()
    xh, xl = split(inverse[...] * scale)
    left = jnp.concatenate([xh, xh, xl], axis=1)
    for c, at in enumerate(spans):
        for copy in loads[c]:
            copy.wait()
        at = pl.ds(*at)
        h = high[:, at]
        q[:, at] = jnp.dot(left, jnp.concatenate([h, low[:, at], h], axis=0), preferred_element_type=F32)
        stores[c].start()
        if c == 0:
            small[1].wait()
            r[...] = upper[...] / scale
            stores.append(pltpu.make_async_copy(r, r_hbm, small_sem.at[2]))
            stores[-1].start()
    for store in stores:
        store.wait()


def shards(n_sx, n_sy, start_block, blocks, neighbors, ghost_lists):
    count_rhs, rows = start_block.shape
    size = 3 * count_rhs
    pairs = rows // 128
    per = 128 // n_sx
    groups = 8
    sum_buffers = [pltpu.VMEM((count, per, 128), F32) for count in (n_sx, n_sx - 1, n_sy, n_sx)]
    anywhere = pl.BlockSpec(memory_space=pl.ANY)
    in_hbm = pl.BlockSpec(memory_space=pltpu.HBM)
    vmem = pl.BlockSpec(memory_space=pltpu.VMEM)
    high, low, upper, inverse = pl.pallas_call(
        functools.partial(basis_kernel, n_sx, n_sy),
        out_shape=(
            jax.ShapeDtypeStruct((size, rows), BF16),
            jax.ShapeDtypeStruct((size, rows), BF16),
            jax.ShapeDtypeStruct((size, size), F32),
            jax.ShapeDtypeStruct((size, size), F32),
        ),
        in_specs=[in_hbm, in_hbm, in_hbm, in_hbm],
        out_specs=(anywhere, anywhere, vmem, vmem),
        scratch_shapes=[
            pltpu.SMEM(neighbors.shape, jnp.int32),
            pltpu.SMEM(ghost_lists.shape, jnp.int32),
            pltpu.VMEM((count_rhs, rows), F32),
            pltpu.VMEM((7, 64, rows), F32),
            pltpu.VMEM((pairs, 512, 256), BF16),
            pltpu.VMEM((96, 2, count_rhs, 128), BF16),
            pltpu.VMEM((96, 2, count_rhs, 128), BF16),
            pltpu.VMEM((size, rows), BF16),
            pltpu.VMEM((size, rows), BF16),
            pltpu.VMEM((2, 4, 4, count_rhs, 128), F32),
            pltpu.VMEM((2, 4, 4, count_rhs, 128), F32),
            *sum_buffers,
            *sum_buffers,
            pltpu.SemaphoreType.DMA((2,)),
            pltpu.SemaphoreType.DMA((4,)),
            pltpu.SemaphoreType.DMA((groups,)),
            pltpu.SemaphoreType.DMA((2,)),
            pltpu.SemaphoreType.DMA((2, 4)),
            pltpu.SemaphoreType.DMA((2, 4)),
            *[pltpu.SemaphoreType.DMA((3,))] * 4,
        ],
        compiler_params=pltpu.CompilerParams(
            collective_id=0, has_side_effects=True, vmem_limit_bytes=56 * 1024 * 1024),
        name="basis_and_factor",
    )(start_block, blocks, neighbors, ghost_lists)

    scale = math.sqrt(rows * n_sx * n_sy)
    cuts = [0, rows // 4, rows // 2, 3 * rows // 4, rows]
    spans = [(low_end, high_end - low_end) for low_end, high_end in zip(cuts[:-1], cuts[1:])]
    parts = len(spans)
    return pl.pallas_call(
        functools.partial(result_kernel, scale, spans),
        out_shape=(jax.ShapeDtypeStruct((size, rows), F32), jax.ShapeDtypeStruct((size, size), F32)),
        in_specs=[anywhere] * 4,
        out_specs=(anywhere, anywhere),
        scratch_shapes=[
            pltpu.VMEM((size, rows), BF16),
            pltpu.VMEM((size, rows), BF16),
            pltpu.VMEM((size, rows), F32),
            pltpu.VMEM((size, size), F32),
            pltpu.VMEM((size, size), F32),
            pltpu.VMEM((size, size), F32),
            pltpu.SemaphoreType.DMA((2, parts)),
            pltpu.SemaphoreType.DMA((parts,)),
            pltpu.SemaphoreType.DMA((3,)),
        ],
        compiler_params=pltpu.CompilerParams(vmem_limit_bytes=56 * 1024 * 1024),
        name="orthonormal_rows",
    )(high, low, upper, inverse)


def solution(mesh):
    return jax.shard_map(
        functools.partial(shards, mesh.shape["sx"], mesh.shape["sy"]),
        mesh=mesh,
        in_specs=(
            P(None, ("sx", "sy")),
            P(None, None, ("sx", "sy")),
            P(None, ("sx", "sy")),
            P("sx", "sy", None, None),
        ),
        out_specs=(P(None, ("sx", "sy")), P()),
        check_vma=False,
    )
```

```python
import functools
import math

import jax
import jax.numpy as jnp
from jax import lax
from jax.experimental import pallas as pl
from jax.experimental.pallas import tpu as pltpu
from jax.sharding import PartitionSpec as P

MESH = pl.DeviceIdType.MESH
F32 = jnp.float32
BF16 = jnp.bfloat16
HIGHEST = lax.Precision.HIGHEST


def split(value):
    high = value.astype(BF16)
    low = (value - high.astype(F32)).astype(BF16)
    return high, low


def exact_dot(a, b, contract):
    return lax.dot_general(a, b, ((contract[0:1], contract[1:2]), ((), ())), precision=HIGHEST, preferred_element_type=F32)


def factor(matrix):
    size = matrix.shape[0]
    shape = (8, 2 * size)
    count = size // 8
    rows = lax.broadcasted_iota(jnp.int32, (size, size), 0)
    cols = lax.broadcasted_iota(jnp.int32, (size, size), 1)
    wide = jnp.concatenate([matrix, jnp.where(rows == cols, 1.0, 0.0).astype(F32)], axis=1)
    parts = [wide[8 * b:8 * b + 8] for b in range(count)]
    sub = lax.broadcasted_iota(jnp.int32, shape, 0)
    lane = lax.broadcasted_iota(jnp.int32, shape, 1)
    done = []
    for t in range(count):
        spread_cols = [[jnp.broadcast_to(parts[b][:, 8 * t + k:8 * t + k + 1], shape) for b in range(t, count)] for k in range(8)]
        spread_rows = [jnp.broadcast_to(parts[t][i:i + 1], shape) for i in range(8)]
        entry = [[jnp.broadcast_to(spread_cols[k][0][i:i + 1], shape) for k in range(i + 1)] for i in range(8)]
        inverse = []
        for j in range(8):
            inverse.append(1.0 / entry[j][j])
            ratio = [None] * 8
            for i in range(j + 1, 8):
                ratio[i] = entry[i][j] * inverse[j]
                for k in range(j + 1, i + 1):
                    entry[i][k] = entry[i][k] - ratio[i] * entry[k][j]
                spread_rows[i] = spread_rows[i] - ratio[i] * spread_rows[j]
                for b in range(1, count - t):
                    spread_cols[i][b] = spread_cols[i][b] - ratio[i] * spread_cols[j][b]
            scaled = spread_rows[j] * inverse[j]
            for b in range(1, count - t):
                parts[t + b] = parts[t + b] - spread_cols[j][b] * scaled
        own = spread_rows[0] / jnp.sqrt(entry[0][0])
        for i in range(1, 8):
            own = jnp.where(sub == i, spread_rows[i] / jnp.sqrt(entry[i][i]), own)
        done.append(jnp.where(lane < sub + 8 * t, 0.0, own))
    result = jnp.concatenate(done, axis=0)
    return result[:, :size], result[:, size:]


def add_up(parts):
    while len(parts) > 1:
        parts = [parts[i] + parts[i + 1] if i + 1 < len(parts) else parts[i] for i in range(0, len(parts), 2)]
    return parts[0]


def ring_hops(d, n):
    return min(d, n - d)


def others_along(sx, sy, n_sx, n_sy):
    n_x = 4 if n_sx == 32 else 1
    n_y = n_sx // (2 * n_x)
    x, y, core = sx // (2 * n_y), (sx // 2) % n_y, sx % 2
    steps = [(dx, dy, dc) for dx in range(n_x) for dy in range(n_y) for dc in range(2)][1:]
    steps.sort(key=lambda step: -(2 * ring_hops(step[0], n_x) + 2 * ring_hops(step[1], n_y) + step[2]))
    along_x = [((lax.rem(x + dx, n_x) * n_y + lax.rem(y + dy, n_y)) * 2 + lax.rem(core + dc, 2)) for dx, dy, dc in steps]
    along_y = [lax.rem(sy + d, n_sy) for d in sorted(range(1, n_sy), key=lambda d: -ring_hops(d, n_sy))]
    same_x = [other for other, step in zip(along_x, steps) if step[0] == 0]
    same_yc = [other for other, step in zip(along_x, steps) if step[1] == step[2] == 0]
    two_off = [lax.rem(sy + d, n_sy) for d in sorted({2 % n_sy, (n_sy - 2) % n_sy} - {0})]
    one_off = [lax.rem(sy + d, n_sy) for d in sorted({1, n_sy - 1})]
    beside = [lax.rem(sx + d, n_sx) for d in (1, n_sx - 1)]
    greeted = [(other, sy) for other in beside + same_yc + same_x] + [(sx, other) for other in one_off + two_off]
    told = [(other, sy) for other in same_x] + [(sx, other) for other in two_off]
    return (along_x, along_y), greeted, told


class SumOverDevices:
    def __init__(self, shape, place, others, refs, send_sem, recv_sem):
        self.n_sx, self.n_sy = shape
        self.sx, self.sy = place
        self.others_x, self.others_y = others
        self.local, self.chunks, self.planes, self.whole = refs
        self.send_sem, self.recv_sem = send_sem, recv_sem

    def send(self, round_, source, target, device):
        pltpu.make_async_remote_copy(
            src_ref=source, dst_ref=target, send_sem=self.send_sem.at[round_], recv_sem=self.recv_sem.at[round_],
            device_id=device, device_id_type=MESH).start()

    def spans(self):
        return (self.chunks, self.planes.at[pl.ds(0, self.n_sy - 1)], self.whole.at[pl.ds(0, self.n_sx - 1)])

    def arrived(self, round_):
        span = self.spans()[round_]
        pltpu.make_async_copy(span, span, self.recv_sem.at[round_]).wait()

    def scatter(self, value):
        self.local[...] = value.reshape(self.local.shape)

        for slot, other in enumerate(self.others_x):
            self.send(0, self.local.at[other], self.chunks.at[slot], (other, self.sy))

    def exchange(self):
        self.arrived(0)
        self.planes[self.sy] = add_up([self.local[self.sx]] + [self.chunks[d] for d in range(self.n_sx - 1)])

        mine = self.planes.at[self.sy]
        for other in self.others_y:
            self.send(1, mine, mine, (self.sx, other))

    def gather(self):
        self.arrived(1)
        self.whole[self.sx] = add_up([self.planes[d] for d in range(self.n_sy)])

        mine = self.whole.at[self.sx]
        for other in self.others_x:
            self.send(2, mine, mine, (other, self.sy))

    def result(self):
        self.arrived(2)
        return self.whole[...].reshape(-1, 128)

    def finish(self):
        for round_, span in enumerate(self.spans()):
            pltpu.make_async_copy(span, span, self.send_sem.at[round_]).wait()


def basis_kernel(n_sx, n_sy, start_hbm, blocks_hbm, near_hbm, lists_hbm, high_hbm, low_hbm, upper_ref, inverse_ref,
                 near_ref, lists_ref, start_vm, stage, tiles, ext_a, ext_b, high, low, send, recv,
                 local_1, chunks_1, planes_1, whole_1, local_2, chunks_2, planes_2, whole_2,
                 index_sem, start_sem, block_sem, out_sem, send_sem, recv_sem, sum_send_1, sum_recv_1, sum_send_2, sum_recv_2, told_sem):
    sx, sy = lax.axis_index("sx"), lax.axis_index("sy")
    count_rhs, rows = start_hbm.shape
    pairs = rows // 128
    groups = block_sem.shape[0]
    width = rows // groups
    per_group = width // 128
    others, greeted, told = others_along(sx, sy, n_sx, n_sy)
    sum_1 = SumOverDevices((n_sx, n_sy), (sx, sy), others, (local_1, chunks_1, planes_1, whole_1), sum_send_1, sum_recv_1)
    sum_2 = SumOverDevices((n_sx, n_sy), (sx, sy), others, (local_2, chunks_2, planes_2, whole_2), sum_send_2, sum_recv_2)

    near_copy = pltpu.make_async_copy(near_hbm, near_ref, index_sem.at[0])
    lists_copy = pltpu.make_async_copy(lists_hbm, lists_ref, index_sem.at[1])
    start_groups = start_sem.shape[0]
    start_width = rows // start_groups
    start_copies = []
    for c in range(start_groups):
        at = pl.ds(c * start_width, start_width)
        copy = pltpu.make_async_copy(start_hbm.at[:, at], start_vm.at[:, at], start_sem.at[c])
        copy.start()
        start_copies.append(copy)
    lists_copy.start()
    near_copy.start()
    block_copies = []
    for c in range(groups):
        copy = pltpu.make_async_copy(blocks_hbm.at[:, :, pl.ds(c * width, width)], stage.at[:, :, pl.ds(c * width, width)], block_sem.at[c])
        copy.start()
        block_copies.append(copy)

    barrier = pltpu.get_barrier_semaphore()

    for device in greeted:
        pl.semaphore_signal(barrier, inc=1, device_id=device, device_id_type=MESH)

    left_half = lax.broadcasted_iota(jnp.int32, (count_rhs, 128), 1) < 64

    def spread(pair, ext, slot):
        turned = pltpu.roll(pair, 64, 1)
        for side, both in enumerate((jnp.where(left_half, pair, turned), jnp.where(left_half, turned, pair))):
            h, l = split(both)
            ext[slot + side, 0] = h
            ext[slot + side, 1] = l

    def keep(pair, p, power):
        h, l = split(pair)
        at = pl.ds(pl.multiple_of(p * 128, 128), 128)
        high[power * count_rhs:(power + 1) * count_rhs, at] = h
        low[power * count_rhs:(power + 1) * count_rhs, at] = l

    def exchange(ext, turn):
        targets = (
            (lax.rem(sx + 1, n_sx), sy),
            (lax.rem(sx + n_sx - 1, n_sx), sy),
            (sx, lax.rem(sy + 1, n_sy)),
            (sx, lax.rem(sy + n_sy - 1, n_sy)),
        )
        copies = {}
        for d in (2, 3, 0, 1):
            for g in range(4):
                first, second = lists_ref[0, 0, d, 2 * g], lists_ref[0, 0, d, 2 * g + 1]
                one = ext[first, 0].astype(F32) + ext[first, 1].astype(F32)
                two = ext[second, 0].astype(F32) + ext[second, 1].astype(F32)
                send[turn, d, g] = jnp.where(left_half, one, two)
            if turn == 0 and d == 2:
                pl.semaphore_wait(barrier, len(greeted))
                for device in told:
                    pl.semaphore_signal(told_sem, inc=1, device_id=device, device_id_type=MESH)
            copy = pltpu.make_async_remote_copy(
                src_ref=send.at[turn, d], dst_ref=recv.at[turn, d],
                send_sem=send_sem.at[turn, d], recv_sem=recv_sem.at[turn, d],
                device_id=targets[d], device_id_type=MESH)
            copy.start()
            copies[d] = copy
        return copies

    def arrive(copies, ext, turn):
        for d in range(4):
            copies[d].wait()
            for g in range(4):
                spread(recv[turn, d, g], ext, 64 + d * 8 + 2 * g)

    def power(ext, use, first_pair, last_pair):
        @pl.loop(first_pair, last_pair, unroll=16)
        def _(p):
            lhs = []
            for hl in range(2):
                for side in range(2):
                    e = 2 * p + side
                    slots = [e] + [near_ref[k, e] for k in range(6)] + [near_ref[5, e]]
                    lhs.append(jnp.concatenate(
                        [jnp.where(left_half, ext[slots[2 * k], hl], ext[slots[2 * k + 1], hl]) for k in range(4)], axis=1))
            out = jnp.dot(jnp.concatenate(lhs, axis=0), tiles[p], preferred_element_type=F32)
            out = out[:, :128] + out[:, 128:]
            out = out[:2 * count_rhs] + out[2 * count_rhs:]
            use(p, jnp.where(left_half, out[:count_rhs], out[count_rhs:]))

    for c in range(start_groups):
        start_copies[c].wait()

        @pl.loop(c * start_width // 128, (c + 1) * start_width // 128, unroll=4)
        def _(p):
            pair = start_vm[:, pl.ds(pl.multiple_of(p * 128, 128), 128)]
            keep(pair, p, 0)
            spread(pair, ext_a, 2 * p)

    lists_copy.wait()
    near_copy.wait()
    copies = exchange(ext_a, 0)

    for c in range(groups):
        block_copies[c].wait()

        @pl.loop(c * per_group, (c + 1) * per_group)
        def _(p):
            at = pl.ds(pl.multiple_of(p * 128, 128), 128)
            for k in range(7):
                h, l = split(stage[k, :, at])
                tiles[p, k * 64:(k + 1) * 64, 0:128] = h
                tiles[p, k * 64:(k + 1) * 64, 128:256] = l
            tiles[p, 448:512, :] = jnp.zeros((64, 256), BF16)

    arrive(copies, ext_a, 0)

    def first(p, pair):
        keep(pair, p, 1)
        spread(pair, ext_b, 2 * p)

    power(ext_a, first, 0, pairs)
    copies = exchange(ext_b, 1)

    depth = 1024
    dims = (((1,), (1,)), ((), ()))

    def products_1(c, total):
        at = pl.ds(pl.multiple_of(c * depth, depth), depth)
        h, l = high[0:2 * count_rhs, at], low[0:2 * count_rhs, at]
        return total + lax.dot_general(h, jnp.concatenate([h, l], axis=0), dims, preferred_element_type=F32)

    total = lax.fori_loop(0, rows // depth, products_1, jnp.zeros((128, 256), F32))
    pl.semaphore_wait(told_sem, len(told))
    sum_1.scatter(total[:, :128] + total[:, 128:] + total[:, 128:].T)

    arrive(copies, ext_b, 1)
    power(ext_b, lambda p, pair: keep(pair, p, 2), 0, pairs // 2)
    sum_1.exchange()
    power(ext_b, lambda p, pair: keep(pair, p, 2), pairs // 2, pairs)

    def products_2(c, totals):
        at = pl.ds(pl.multiple_of(c * depth, depth), depth)
        new = jnp.concatenate([high[128:192, at], low[128:192, at]], axis=0)
        old = jnp.concatenate([high[0:128, at], low[0:128, at]], axis=0)
        return (totals[0] + lax.dot_general(new, old, dims, preferred_element_type=F32),
                totals[1] + lax.dot_general(new, new, dims, preferred_element_type=F32))

    across, corner = lax.fori_loop(0, rows // depth, products_2, (jnp.zeros((128, 256), F32), jnp.zeros((128, 128), F32)))
    across = across[:64, :128] + across[:64, 128:] + across[64:, :128]
    corner = corner[:64, :64] + corner[:64, 64:] + corner[64:, :64]
    sum_2.scatter(jnp.concatenate([across, jnp.concatenate([corner, jnp.zeros((64, 64), F32)], axis=1)], axis=0))

    out_copies = [pltpu.make_async_copy(high, high_hbm, out_sem.at[0]), pltpu.make_async_copy(low, low_hbm, out_sem.at[1])]
    for copy in out_copies:
        copy.start()

    sum_1.gather()
    sum_2.exchange()
    none = jnp.zeros((64, 64), F32)
    full = sum_1.result()
    u00, x00 = factor(full[0:64, 0:64])
    u01 = exact_dot(x00, full[0:64, 64:128], (1, 0))
    s11 = full[64:128, 64:128] - exact_dot(u01, u01, (0, 0))
    sum_2.gather()
    u11, x11 = factor(s11)
    x10 = -exact_dot(x11, exact_dot(u01, x00, (0, 0)), (1, 0))
    x1 = jnp.concatenate([jnp.concatenate([x00, none], axis=1), jnp.concatenate([x10, x11], axis=1)], axis=0)
    upper_ref[0:64, 0:128] = jnp.concatenate([u00, u01], axis=1)
    upper_ref[64:128, 0:128] = jnp.concatenate([none, u11], axis=1)
    upper_ref[128:192, 0:128] = jnp.zeros((64, 128), F32)
    inverse_ref[0:128, 0:128] = x1
    inverse_ref[0:128, 128:192] = jnp.zeros((128, 64), F32)

    full = sum_2.result()
    u2 = exact_dot(x1, full[0:64], (1, 1))
    u22, x22 = factor(full[64:128, 0:64] - exact_dot(u2, u2, (0, 0)))
    inverse_ref[128:192, 0:128] = -exact_dot(x22, exact_dot(u2, x1, (0, 0)), (1, 0))
    inverse_ref[128:192, 128:192] = x22
    upper_ref[0:128, 128:192] = u2
    upper_ref[128:192, 128:192] = u22

    for copy in out_copies:
        copy.wait()
    sum_1.finish()
    sum_2.finish()


def result_kernel(scale, spans, high_hbm, low_hbm, upper_hbm, inverse_hbm, q_hbm, r_hbm, high, low, q, upper, inverse, r, in_sem, out_sem, small_sem):
    loads, stores = [], []
    for c, at in enumerate(spans):
        at = pl.ds(*at)
        loads.append((pltpu.make_async_copy(high_hbm.at[:, at], high.at[:, at], in_sem.at[0, c]),
                      pltpu.make_async_copy(low_hbm.at[:, at], low.at[:, at], in_sem.at[1, c])))
        stores.append(pltpu.make_async_copy(q.at[:, at], q_hbm.at[:, at], out_sem.at[c]))
    small = [pltpu.make_async_copy(inverse_hbm, inverse, small_sem.at[0]), pltpu.make_async_copy(upper_hbm, upper, small_sem.at[1])]
    small[0].start()
    for pair in loads:
        for copy in pair:
            copy.start()
    small[1].start()
    small[0].wait()
    xh, xl = split(inverse[...] * scale)
    for c, at in enumerate(spans):
        for copy in loads[c]:
            copy.wait()
        at = pl.ds(*at)
        h = high[:, at]
        l = low[:, at]
        q[:, at] = (jnp.dot(xh, h, preferred_element_type=F32) + jnp.dot(xh, l, preferred_element_type=F32)
                    + jnp.dot(xl, h, preferred_element_type=F32))
        stores[c].start()
        if c == 0:
            small[1].wait()
            r[...] = upper[...] / scale
            stores.append(pltpu.make_async_copy(r, r_hbm, small_sem.at[2]))
            stores[-1].start()
    for store in stores:
        store.wait()


def shards(n_sx, n_sy, start_block, blocks, neighbors, ghost_lists):
    count_rhs, rows = start_block.shape
    size = 3 * count_rhs
    pairs = rows // 128
    per = 128 // n_sx
    groups = 8
    sum_buffers = [pltpu.VMEM((count, per, 128), F32) for count in (n_sx, n_sx - 1, n_sy, n_sx)]
    anywhere = pl.BlockSpec(memory_space=pl.ANY)
    in_hbm = pl.BlockSpec(memory_space=pltpu.HBM)
    vmem = pl.BlockSpec(memory_space=pltpu.VMEM)
    high, low, upper, inverse = pl.pallas_call(
        functools.partial(basis_kernel, n_sx, n_sy),
        out_shape=(
            jax.ShapeDtypeStruct((size, rows), BF16),
            jax.ShapeDtypeStruct((size, rows), BF16),
            jax.ShapeDtypeStruct((size, size), F32),
            jax.ShapeDtypeStruct((size, size), F32),
        ),
        in_specs=[in_hbm, in_hbm, in_hbm, in_hbm],
        out_specs=(anywhere, anywhere, vmem, vmem),
        scratch_shapes=[
            pltpu.SMEM(neighbors.shape, jnp.int32),
            pltpu.SMEM(ghost_lists.shape, jnp.int32),
            pltpu.VMEM((count_rhs, rows), F32),
            pltpu.VMEM((7, 64, rows), F32),
            pltpu.VMEM((pairs, 512, 256), BF16),
            pltpu.VMEM((96, 2, count_rhs, 128), BF16),
            pltpu.VMEM((96, 2, count_rhs, 128), BF16),
            pltpu.VMEM((size, rows), BF16),
            pltpu.VMEM((size, rows), BF16),
            pltpu.VMEM((2, 4, 4, count_rhs, 128), F32),
            pltpu.VMEM((2, 4, 4, count_rhs, 128), F32),
            *sum_buffers,
            *sum_buffers,
            pltpu.SemaphoreType.DMA((2,)),
            pltpu.SemaphoreType.DMA((4,)),
            pltpu.SemaphoreType.DMA((groups,)),
            pltpu.SemaphoreType.DMA((2,)),
            pltpu.SemaphoreType.DMA((2, 4)),
            pltpu.SemaphoreType.DMA((2, 4)),
            *[pltpu.SemaphoreType.DMA((3,))] * 4,
            pltpu.SemaphoreType.REGULAR,
        ],
        compiler_params=pltpu.CompilerParams(
            collective_id=0, has_side_effects=True, vmem_limit_bytes=56 * 1024 * 1024),
        name="basis_and_factor",
    )(start_block, blocks, neighbors, ghost_lists)

    scale = math.sqrt(rows * n_sx * n_sy)
    cuts = [0, rows // 4, rows // 2, 3 * rows // 4, rows]
    spans = [(low_end, high_end - low_end) for low_end, high_end in zip(cuts[:-1], cuts[1:])]
    parts = len(spans)
    return pl.pallas_call(
        functools.partial(result_kernel, scale, spans),
        out_shape=(jax.ShapeDtypeStruct((size, rows), F32), jax.ShapeDtypeStruct((size, size), F32)),
        in_specs=[anywhere] * 4,
        out_specs=(anywhere, anywhere),
        scratch_shapes=[
            pltpu.VMEM((size, rows), BF16),
            pltpu.VMEM((size, rows), BF16),
            pltpu.VMEM((size, rows), F32),
            pltpu.VMEM((size, size), F32),
            pltpu.VMEM((size, size), F32),
            pltpu.VMEM((size, size), F32),
            pltpu.SemaphoreType.DMA((2, parts)),
            pltpu.SemaphoreType.DMA((parts,)),
            pltpu.SemaphoreType.DMA((3,)),
        ],
        compiler_params=pltpu.CompilerParams(vmem_limit_bytes=56 * 1024 * 1024),
        name="orthonormal_rows",
    )(high, low, upper, inverse)


def solution(mesh):
    return jax.shard_map(
        functools.partial(shards, mesh.shape["sx"], mesh.shape["sy"]),
        mesh=mesh,
        in_specs=(
            P(None, ("sx", "sy")),
            P(None, None, ("sx", "sy")),
            P(None, ("sx", "sy")),
            P("sx", "sy", None, None),
        ),
        out_specs=(P(None, ("sx", "sy")), P()),
        check_vma=False,
    )
```
